256 devices in a mesh: seq: 32 (over z, x), vocab: 8 (over y, core).
Axes of the slice: x: 4, y: 4, z: 8, core: 2. Of those that a mesh axis runs over, the one named last changes fastest.
Arguments:
- rollout: bfloat16 [1152, 4096], P('seq')
- group_count: int32 [32], replicated, may hold values from 12 to 36, as said below
- final_gain: float32 [4096], replicated, may hold values from 0.5 to 1.5
- head_weight: bfloat16 [4096, 152064], P(None, ('seq', 'vocab'))
- teacher_index: int32 [768, 64], replicated, may hold values from 0 to 152063, as said below
- teacher_logprob: float32 [768, 64], replicated, as said below
Outputs:
- kl: float32 [768], P('seq')
- grad_weight: bfloat16 [4096, 152064], P(None, ('seq', 'vocab'))
- grad_rollout: bfloat16 [1152, 4096], P('seq', 'vocab')
The draws below stay inside these ranges and needn't reach their ends.
Inputs may be any that keep to these rules, and one draw needn't show every extreme that they name: The first group_count[g] of the 36 slots of group g are live, the rest padding; the counts sum to 768. `teacher_index`: the 64 ids of one token are distinct. `teacher_logprob`: the exponentials of one token's entries sum to less than 1.
All inputs are finite; a program needn't handle non-finite values.
Results may differ from the reference program's by a relative error of at most 0.0075.
Values may be sent and summed in bfloat16 or wider, within the bound.
No kernel may reach another device: no remote copies, remote signals or barrier semaphores. Data moves between devices by JAX's collectives and lax.ppermute only.
A program may use at most 128 MiB of HBM per device.

```python
import math
import jax
import jax.numpy as jnp
from jax import lax

D = 4096
VOCAB = 152064
TOPK = 64
PACK_DEV = 24
SLOT_DEV = 36
TOKENS = 768
GEN_SLOTS = 1152
N_SEQ = 32


def drawn_columns(key):
    inner = jax.random.fold_in(key, 7)
    columns = 2 * jax.random.randint(jax.random.fold_in(inner, 1), (4,), 0, VOCAB // 2)
    vectors = jax.random.uniform(jax.random.fold_in(inner, 2), (4, D), jnp.float32, -1.0, 1.0) * math.sqrt(3.0)
    return (columns, vectors)


def draw_head_weight(key, part):
    spread = 3.5 / math.sqrt(D)
    table = jax.random.normal(key, (D, VOCAB), jnp.float32) * spread
    table = jnp.clip(table, -5.5 * spread, 5.5 * spread)
    columns, vectors = drawn_columns(key)
    strong = 320.0 / D * vectors.T
    table = table.at[:, columns].set(strong)
    table = table.at[:, columns + 1].set(0.993 * strong)
    return table.astype(jnp.bfloat16)


def draw_rollout(key, part):
    table = jax.random.normal(key, (GEN_SLOTS, D), jnp.float32)
    columns, vectors = drawn_columns(key)
    picker = jax.random.fold_in(key, 5)
    chosen_group = jax.random.randint(jax.random.fold_in(picker, 1), (8,), 0, GEN_SLOTS // SLOT_DEV)
    chosen_row = jax.random.randint(jax.random.fold_in(picker, 2), (8,), 0, PACK_DEV // 2)
    row_ids = chosen_group * SLOT_DEV + chosen_row
    strength = jnp.array([0.5, 1.0, 2.0, 4.0, 0.5, 1.0, 2.0, 4.0], jnp.float32)[:, None]
    which = jnp.arange(8) % 4
    table = table.at[row_ids].set(table[row_ids] + strength * vectors[which])
    return table.astype(jnp.bfloat16)


def draw_group_count(key, part):
    group_total = GEN_SLOTS // SLOT_DEV
    half_pack = PACK_DEV // 2
    group_order = jax.random.permutation(jax.random.fold_in(key, 11), group_total)
    shift_size = jax.random.randint(jax.random.fold_in(key, 12), (group_total // 2,), -(half_pack - 1), half_pack)
    shift_size = shift_size.at[0].set(half_pack)
    counts = jnp.zeros((group_total,), jnp.int32)
    counts = counts.at[group_order[0::2]].set(PACK_DEV + shift_size)
    counts = counts.at[group_order[1::2]].set(PACK_DEV - shift_size)
    return counts.astype(jnp.int32)


def draw_teacher_index(key, part):
    row_keys = jax.random.split(jax.random.fold_in(key, 21), TOKENS)
    residues = jax.vmap(lambda row_key: jax.random.permutation(row_key, TOPK))(row_keys)
    bucket = jax.random.randint(jax.random.fold_in(key, 22), (TOKENS, TOPK), 0, VOCAB // TOPK)
    return (bucket * TOPK + residues).astype(jnp.int32)


def draw_teacher_logprob(key, part):
    raw = 2.0 * jax.random.normal(key, (TOKENS, TOPK), jnp.float32)
    teacher_mass = jax.random.uniform(jax.random.fold_in(key, 31), (TOKENS, 1), jnp.float32, 0.5, 0.98)
    result = raw - jax.nn.logsumexp(raw, axis=1, keepdims=True) + jnp.log(teacher_mass)
    return result.astype(jnp.float32)


def setup_inputs(seed: int = 0) -> dict:
    keys = jax.random.split(jax.random.key(seed), 7)
    return {
        "rollout": draw_rollout(jax.random.fold_in(keys[6], 71), 0),
        "group_count": draw_group_count(jax.random.fold_in(keys[6], 71), 0),
        "final_gain": jnp.clip(1.0 + 0.1 * jax.random.normal(keys[2], (D,), jnp.float32), 0.5, 1.5),
        "head_weight": draw_head_weight(jax.random.fold_in(keys[6], 71), 0),
        "teacher_index": draw_teacher_index(jax.random.fold_in(keys[6], 71), 0),
        "teacher_logprob": draw_teacher_logprob(jax.random.fold_in(keys[6], 71), 0),
    }


norm_eps = 1e-06
loss_scale = 16.0

def pack_index(group_count):
    offsets = jnp.cumsum(group_count) - group_count
    row_ids = jnp.arange(SLOT_DEV, dtype=jnp.int32)
    rank = offsets[:, None] + row_ids[None, :]
    is_live = row_ids[None, :] < group_count[:, None]
    target = rank % N_SEQ * PACK_DEV + rank // N_SEQ
    target = jnp.where(is_live, target, TOKENS).astype(jnp.int32)
    return (target.reshape(-1), is_live.reshape(-1))

def reference(rollout, group_count, final_gain, head_weight, teacher_index, teacher_logprob):
    target, is_live = pack_index(group_count)
    packed = jnp.zeros((TOKENS, D), rollout.dtype).at[target].set(rollout, mode='drop')
    values = packed.astype(jnp.float32)
    inv_rms = lax.rsqrt(lax.optimization_barrier(jnp.mean(values * values, axis=1, keepdims=True)) + norm_eps)
    normed = (values * inv_rms * final_gain).astype(jnp.bfloat16)
    teacher_prob = jnp.exp(teacher_logprob)
    teacher_mass = lax.optimization_barrier(jnp.sum(teacher_prob, axis=1))
    block_width = VOCAB // 64
    block_ids = jnp.arange(64, dtype=jnp.int32)
    token_ids = jnp.arange(TOKENS, dtype=jnp.int32)[:, None]

    def block_logits(block_id):
        start = (block_id * block_width).astype(jnp.int32)
        weight_block = lax.dynamic_slice_in_dim(head_weight, start, block_width, 1)
        logits = jnp.dot(normed, weight_block, preferred_element_type=jnp.float32)
        local = teacher_index - start
        owned = (local >= 0) & (local < block_width)
        return (weight_block, logits, local, owned)

    def first_pass(carry, block_id):
        row_peak, row_total, target_sum = carry
        weight_block, logits, local, owned = block_logits(block_id)
        new_peak = jnp.maximum(row_peak, lax.optimization_barrier(jnp.max(logits, axis=1)))
        row_total = row_total * jnp.exp(row_peak - new_peak) + lax.optimization_barrier(jnp.sum(jnp.exp(logits - new_peak[:, None]), axis=1))
        picked = jnp.take_along_axis(logits, jnp.clip(local, 0, block_width - 1), axis=1)
        target_sum = target_sum + lax.optimization_barrier(jnp.sum(jnp.where(owned, teacher_prob * picked, 0.0), axis=1))
        return ((new_peak, row_total, target_sum), None)
    start_carry = (jnp.full((TOKENS,), -jnp.inf, jnp.float32), jnp.zeros((TOKENS,), jnp.float32), jnp.zeros((TOKENS,), jnp.float32))
    (row_peak, row_total, target_sum), _ = lax.scan(first_pass, start_carry, block_ids)
    log_total = row_peak + jnp.log(row_total)
    kl = lax.optimization_barrier(jnp.sum(teacher_prob * teacher_logprob, axis=1)) - target_sum + teacher_mass * log_total

    def second_pass(grad_normed, block_id):
        weight_block, logits, local, owned = block_logits(block_id)
        student_part = teacher_mass[:, None] * jnp.exp(logits - log_total[:, None])
        column = jnp.where(owned, local, block_width)
        student_part = student_part.at[token_ids, column].add(-teacher_prob, mode='drop')
        grad_logits = (loss_scale * student_part).astype(jnp.bfloat16)
        grad_block = lax.dot_general(normed, grad_logits, (((0,), (0,)), ((), ())), preferred_element_type=jnp.float32).astype(jnp.bfloat16)
        grad_normed = grad_normed + lax.dot_general(grad_logits, weight_block, (((1,), (1,)), ((), ())), preferred_element_type=jnp.float32)
        return (grad_normed, grad_block)
    grad_normed, grad_blocks = lax.scan(second_pass, jnp.zeros((TOKENS, D), jnp.float32), block_ids)
    grad_weight = grad_blocks.transpose(1, 0, 2).reshape(D, VOCAB)
    scaled_grad = grad_normed * final_gain
    row_dots = lax.optimization_barrier(jnp.sum(scaled_grad * values, axis=1, keepdims=True))
    grad_packed = ((scaled_grad - values * inv_rms * inv_rms * row_dots / D) * inv_rms).astype(jnp.bfloat16)
    gathered = jnp.take(grad_packed, jnp.minimum(target, TOKENS - 1), axis=0)
    grad_rollout = jnp.where(is_live[:, None], gathered, jnp.zeros_like(gathered))
    return (kl, grad_weight, grad_rollout)
```

```python
import jax
import jax.numpy as jnp
from jax import lax
from jax.experimental import pallas as pl
from jax.experimental.pallas import tpu as pltpu
from jax.sharding import PartitionSpec as P

norm_eps = 1e-06
loss_scale = 16.0
f32, bf16 = jnp.float32, jnp.bfloat16

NX, NY, NZ = 4, 4, 8
GROUPS = NX * NZ
X_LINES = [[z * NX + x for x in range(NX)] for z in range(NZ)]
Z_LINES = [[z * NX + x for z in range(NZ)] for x in range(NX)]
Y_LINES = [[y * 2 + core for y in range(NY)] for core in range(2)]
OTHER_CORE = [(i, i ^ 1) for i in range(2 * NY)]
VMEM = 48 * 2**20


def params():
    return pltpu.CompilerParams(vmem_limit_bytes=VMEM)


def teacher_kernel(first_ref, index_ref, logprob_ref, dense_ref):
    local = index_ref[...] - first_ref[0]
    prob = jnp.exp(logprob_ref[...])
    rows, entries = local.shape
    lanes = lax.broadcasted_iota(jnp.int32, dense_ref.shape, 1)
    dense = jnp.zeros(dense_ref.shape, f32)
    for j in range(entries):
        dense = jnp.where(local[:, j : j + 1] == lanes, prob[:, j : j + 1], dense)
    dense_ref[...] = dense


def teacher_rows(first_column, index, logprob, width):
    tokens, entries = index.shape
    block = 64
    return pl.pallas_call(
        teacher_kernel,
        grid_spec=pltpu.PrefetchScalarGridSpec(
            num_scalar_prefetch=1,
            grid=(tokens // block,),
            in_specs=[pl.BlockSpec((block, entries), lambda i, s: (i, 0))] * 2,
            out_specs=pl.BlockSpec((block, width), lambda i, s: (i, 0)),
        ),
        out_shape=jax.ShapeDtypeStruct((tokens, width), f32),
        cost_estimate=pl.CostEstimate(flops=3 * tokens * width * entries, bytes_accessed=4 * tokens * width, transcendentals=0),
        compiler_params=params(),
        name="teacher_rows",
    )(first_column.reshape(1), index, logprob)


def logits_own_kernel(block_ref, rows_ref, weight_ref, out_ref):
    part = jnp.dot(rows_ref[0], weight_ref[...], preferred_element_type=f32)

    @pl.when(pl.program_id(0) == 0)
    def _():
        out_ref[...] = part

    @pl.when(pl.program_id(0) > 0)
    def _():
        out_ref[...] += part


def logits_rest_kernel(block_ref, rows_ref, weight_ref, own_ref, dense_ref, out_ref, stats_ref):
    part = jnp.dot(rows_ref[0], weight_ref[...], preferred_element_type=f32)

    @pl.when(pl.program_id(0) == 0)
    def _():
        out_ref[...] = own_ref[...] + part

    @pl.when(pl.program_id(0) > 0)
    def _():
        out_ref[...] += part

    @pl.when(pl.program_id(0) == pl.num_programs(0) - 1)
    def _():
        step = 128
        lanes = lax.broadcasted_iota(jnp.int32, (step, 128), 1)
        for i in range(0, out_ref.shape[0], step):
            logits = out_ref[i : i + step, :]
            peak = jnp.max(logits, axis=1, keepdims=True)
            total = peak + jnp.log(jnp.sum(jnp.exp(logits - peak), axis=1, keepdims=True))
            target = jnp.sum(logits * dense_ref[i : i + step, :], axis=1, keepdims=True)
            both = jnp.where(lanes == 0, total, jnp.where(lanes == 1, target, 0.0))
            stats_ref[:, i : i + step] = both.T[: stats_ref.shape[0], :]


def logits_own(blocks, rows, weight):
    count, tokens, share = rows.shape
    width = weight.shape[1]
    return pl.pallas_call(
        logits_own_kernel,
        grid_spec=pltpu.PrefetchScalarGridSpec(
            num_scalar_prefetch=1,
            grid=(count,),
            in_specs=[
                pl.BlockSpec((1, tokens, share), lambda k, b: (k, 0, 0)),
                pl.BlockSpec((share, width), lambda k, b: (b[k], 0)),
            ],
            out_specs=pl.BlockSpec((tokens, width), lambda k, b: (0, 0)),
        ),
        out_shape=jax.ShapeDtypeStruct((tokens, width), f32),
        cost_estimate=pl.CostEstimate(flops=2 * count * tokens * share * width, bytes_accessed=8 * 2**20, transcendentals=0),
        compiler_params=params(),
        name="logits_own",
    )(blocks, rows, weight)


def logits_rest(blocks, rows, weight, own, dense):
    count, tokens, share = rows.shape
    width = weight.shape[1]
    whole = pl.BlockSpec((tokens, width), lambda k, b: (0, 0))
    return pl.pallas_call(
        logits_rest_kernel,
        grid_spec=pltpu.PrefetchScalarGridSpec(
            num_scalar_prefetch=1,
            grid=(count,),
            in_specs=[
                pl.BlockSpec((1, tokens, share), lambda k, b: (k, 0, 0)),
                pl.BlockSpec((share, width), lambda k, b: (b[k], 0)),
                whole,
                whole,
            ],
            out_specs=[whole, pl.BlockSpec((8, tokens), lambda k, b: (0, 0))],
        ),
        out_shape=[jax.ShapeDtypeStruct((tokens, width), f32), jax.ShapeDtypeStruct((8, tokens), f32)],
        cost_estimate=pl.CostEstimate(flops=2 * count * tokens * share * width, bytes_accessed=12 * 2**20, transcendentals=0),
        compiler_params=params(),
        name="logits_rest",
    )(blocks, rows, weight, own, dense)


def times_weight(grad, weight):
    return lax.dot_general(grad, weight, (((1,), (1,)), ((), ())), preferred_element_type=f32)


def grad_rest_kernel(block_ref, totals_ref, logits_ref, dense_ref, logprob_ref, weight_ref, grad_ref, out_ref):
    @pl.when(pl.program_id(0) == 0)
    def _():
        step = 128
        for i in range(0, logits_ref.shape[0], step):
            totals = totals_ref[:, i : i + step]
            peak = jnp.max(totals, axis=0, keepdims=True)
            total = peak + jnp.log(jnp.sum(jnp.exp(totals - peak), axis=0, keepdims=True))
            column = jnp.broadcast_to(total, (128, step)).T[:, :1]
            mass = jnp.sum(jnp.exp(logprob_ref[i : i + step, :]), axis=1, keepdims=True)
            student = mass * jnp.exp(logits_ref[i : i + step, :] - column)
            grad_ref[i : i + step, :] = (loss_scale * (student - dense_ref[i : i + step, :])).astype(bf16)

    out_ref[0] = times_weight(grad_ref[...], weight_ref[...]).astype(bf16)


def grad_rest(blocks, totals, logits, dense, logprob, weight):
    tokens, width = logits.shape
    count = blocks.shape[0]
    share = weight.shape[0] // (2 * count)
    whole = pl.BlockSpec((tokens, width), lambda k, b: (0, 0))
    return pl.pallas_call(
        grad_rest_kernel,
        grid_spec=pltpu.PrefetchScalarGridSpec(
            num_scalar_prefetch=1,
            grid=(count,),
            in_specs=[
                pl.BlockSpec(totals.shape, lambda k, b: (0, 0)),
                whole,
                whole,
                pl.BlockSpec(logprob.shape, lambda k, b: (0, 0)),
                pl.BlockSpec((share, width), lambda k, b: (b[k], 0)),
            ],
            out_specs=[whole, pl.BlockSpec((1, tokens, share), lambda k, b: (k, 0, 0))],
        ),
        out_shape=[jax.ShapeDtypeStruct((tokens, width), bf16), jax.ShapeDtypeStruct((count, tokens, share), bf16)],
        cost_estimate=pl.CostEstimate(flops=2 * count * tokens * share * width, bytes_accessed=12 * 2**20, transcendentals=0),
        compiler_params=params(),
        name="grad_rest",
    )(blocks, totals, logits, dense, logprob, weight)


def grad_own_kernel(block_ref, grad_ref, weight_ref, other_ref, out_ref):
    out_ref[0] = (times_weight(grad_ref[...], weight_ref[...]) + other_ref[0].astype(f32)).astype(bf16)


def grad_own(blocks, grad, weight, other):
    count, tokens, share = other.shape
    width = weight.shape[1]
    piece = pl.BlockSpec((1, tokens, share), lambda k, b: (k, 0, 0))
    return pl.pallas_call(
        grad_own_kernel,
        grid_spec=pltpu.PrefetchScalarGridSpec(
            num_scalar_prefetch=1,
            grid=(count,),
            in_specs=[
                pl.BlockSpec((tokens, width), lambda k, b: (0, 0)),
                pl.BlockSpec((share, width), lambda k, b: (b[k], 0)),
                piece,
            ],
            out_specs=piece,
        ),
        out_shape=jax.ShapeDtypeStruct(other.shape, bf16),
        cost_estimate=pl.CostEstimate(flops=2 * count * tokens * share * width, bytes_accessed=12 * 2**20, transcendentals=0),
        compiler_params=params(),
        name="grad_own",
    )(blocks, grad, weight, other)


def weight_grad_kernel(block_ref, own_ref, rest_ref, grad_ref, out_ref):
    def write(rows):
        out_ref[...] = lax.dot_general(
            rows, grad_ref[...], (((0,), (0,)), ((), ())), preferred_element_type=f32
        ).astype(bf16)

    half = pl.num_programs(0) // 2

    @pl.when(pl.program_id(0) < half)
    def _():
        write(own_ref[0])

    @pl.when(pl.program_id(0) >= half)
    def _():
        write(rest_ref[0])


def weight_grad(blocks, own, rest, grad):
    count, tokens, share = own.shape
    width = grad.shape[1]
    return pl.pallas_call(
        weight_grad_kernel,
        grid_spec=pltpu.PrefetchScalarGridSpec(
            num_scalar_prefetch=1,
            grid=(2 * count,),
            in_specs=[
                pl.BlockSpec((1, tokens, share), lambda k, b: (jnp.minimum(k, count - 1), 0, 0)),
                pl.BlockSpec((1, tokens, share), lambda k, b: (jnp.maximum(k - count, 0), 0, 0)),
                pl.BlockSpec((tokens, width), lambda k, b: (0, 0)),
            ],
            out_specs=pl.BlockSpec((share, width), lambda k, b: (b[k], 0)),
        ),
        out_shape=jax.ShapeDtypeStruct((2 * count * share, width), bf16),
        cost_estimate=pl.CostEstimate(flops=4 * count * tokens * share * width, bytes_accessed=12 * 2**20, transcendentals=0),
        compiler_params=params(),
        name="weight_grad",
    )(blocks, own, rest, grad)


def exchange(x, axis, lines=None):
    return lax.all_to_all(x, axis, 0, 0, tiled=True, axis_index_groups=lines)


def to_all(x, count):
    return jnp.broadcast_to(x[None], (count, *x.shape))


def per_device(rollout, group_count, final_gain, head_weight, teacher_index, teacher_logprob):
    slots, features = rollout.shape
    tokens, entries = teacher_index.shape
    width = head_weight.shape[1]
    parts = 2 * NY
    share = features // parts
    class_rows = tokens // NX
    turns = slots // NX
    pack_rows = tokens // GROUPS
    seq = lax.axis_index("seq")
    own_z, own_x = seq // NX, seq % NX
    vocab = lax.axis_index("vocab")
    core = vocab % 2
    feature_start = vocab * share

    group_ids = jnp.arange(GROUPS, dtype=jnp.int32)
    before = group_ids[None, :] < group_ids[:, None]
    offsets = jnp.sum(jnp.where(before, group_count[None, :], 0), axis=1)
    own_offset = offsets[seq]
    own_count = group_count[seq]
    turn_ids = jnp.arange(turns, dtype=jnp.int32)

    values = rollout.astype(f32)
    inv_rms = lax.rsqrt(jnp.mean(values * values, axis=1, keepdims=True) + norm_eps)
    x_share = lax.dynamic_slice_in_dim(rollout, feature_start, share, 1).astype(f32)
    gain_share = lax.dynamic_slice_in_dim(final_gain, feature_start, share, 0)
    normed = (x_share * inv_rms * gain_share).astype(bf16)
    class_ids = jnp.arange(NX, dtype=jnp.int32)
    source_row = ((class_ids[:, None] - own_offset) % NX + NX * turn_ids[None, :]).reshape(-1)
    slot_ids = jnp.arange(slots, dtype=jnp.int32)
    sort_rows = ((source_row[:, None] == slot_ids[None, :]) & (source_row < own_count)[:, None]).astype(bf16)
    by_class = jnp.dot(sort_rows, normed, preferred_element_type=f32).astype(bf16)
    of_class = exchange(by_class.reshape(NX, turns, share), "seq", X_LINES)
    of_class = exchange(to_all(of_class.reshape(slots, share), NZ), "seq", Z_LINES)

    row_in_group = (own_x - offsets[:, None]) % NX + NX * turn_ids[None, :]
    place = jnp.where(row_in_group < group_count[:, None], (offsets[:, None] + row_in_group) // NX, class_rows)
    place = place.reshape(-1)
    place_ids = jnp.arange(class_rows, dtype=jnp.int32)
    spread = (place[:, None] == place_ids[None, :]).astype(bf16)
    dense_rows = lax.dot_general(
        spread, of_class.reshape(-1, share), (((0,), (0,)), ((), ())), preferred_element_type=f32
    ).astype(bf16)
    all_x = exchange(to_all(dense_rows, NX), "seq", X_LINES).reshape(tokens, share)
    own_rows = exchange(to_all(all_x, NY), "vocab", Y_LINES)
    rest_rows = lax.ppermute(own_rows, "vocab", OTHER_CORE)

    def class_order(a):
        return a.reshape(NZ, NX, pack_rows, entries).transpose(1, 2, 0, 3).reshape(tokens, entries)

    index = class_order(teacher_index)
    logprob = class_order(teacher_logprob)
    first_column = (seq * parts + vocab) * width
    dense = teacher_rows(first_column, index, logprob, width)

    y_ids = jnp.arange(NY, dtype=jnp.int32)
    own_blocks = 2 * y_ids + core
    rest_blocks = 2 * y_ids + 1 - core
    logits_part = logits_own(own_blocks, own_rows, head_weight)
    logits, stats = logits_rest(rest_blocks, rest_rows, head_weight, logits_part, dense)
    stats = exchange(to_all(stats[:2], parts), "vocab")
    peak = jnp.max(stats[:, 0], axis=0)
    part_total = peak + jnp.log(jnp.sum(jnp.exp(stats[:, 0] - peak), axis=0))
    part_target = jnp.sum(stats[:, 1], axis=0)
    stats = exchange(to_all(jnp.stack([part_total, part_target]), GROUPS), "seq")
    totals = stats[:, 0]

    grad, rest_grad = grad_rest(rest_blocks, totals, logits, dense, logprob, head_weight)
    other_grad = lax.ppermute(rest_grad, "vocab", OTHER_CORE)
    chip_grad = grad_own(own_blocks, grad, head_weight, other_grad)
    grad_weight = weight_grad(jnp.concatenate([own_blocks, rest_blocks]), own_rows, rest_rows, grad)

    y_grad = jnp.sum(exchange(chip_grad, "vocab", Y_LINES).astype(f32), axis=0).astype(bf16)
    x_grad = jnp.sum(
        exchange(y_grad.reshape(NX, class_rows, share), "seq", X_LINES).astype(f32), axis=0
    ).astype(bf16)
    spread_grad = jnp.dot(spread, x_grad, preferred_element_type=f32).astype(bf16)
    z_grad = jnp.sum(exchange(spread_grad.reshape(NZ, slots, share), "seq", Z_LINES).astype(f32), axis=0)
    sorted_grad = exchange(z_grad.reshape(NX, turns, share), "seq", X_LINES).reshape(slots, share)
    from_row = (own_offset + slot_ids) % NX * turns + slot_ids // NX
    grad_normed = jnp.take(sorted_grad, from_row, axis=0)

    u = grad_normed * gain_share
    row_dots = jnp.sum(exchange(to_all(jnp.sum(u * x_share, axis=1), parts), "vocab"), axis=0)[:, None]
    grad_rows = (u - x_share * inv_rms * inv_rms * row_dots / features) * inv_rms
    grad_rollout = jnp.where((slot_ids < own_count)[:, None], grad_rows, 0.0).astype(bf16)

    peak = jnp.max(totals, axis=0)
    log_total = peak + jnp.log(jnp.sum(jnp.exp(totals - peak), axis=0))
    target = jnp.sum(stats[:, 1], axis=0)
    prob = jnp.exp(logprob)
    kl_all = jnp.sum(prob * logprob, axis=1) - target + jnp.sum(prob, axis=1) * log_total
    kl_x = lax.dynamic_slice_in_dim(kl_all, own_x * class_rows, class_rows).reshape(pack_rows, NZ)
    kl = jnp.sum(jnp.where(jnp.arange(NZ)[None, :] == own_z, kl_x, 0.0), axis=1)
    return (kl, grad_weight, grad_rollout)


def solution(mesh):
    placed = (P("seq", None), P(), P(), P(None, ("seq", "vocab")), P(), P())
    return jax.shard_map(
        per_device,
        mesh=mesh,
        in_specs=placed,
        out_specs=(P("seq"), P(None, ("seq", "vocab")), P("seq", "vocab")),
        check_vma=False,
    )
```

```python
import jax
import jax.numpy as jnp
from jax import lax
from jax.experimental import pallas as pl
from jax.experimental.pallas import tpu as pltpu
from jax.sharding import PartitionSpec as P

norm_eps = 1e-06
loss_scale = 16.0
f32, bf16 = jnp.float32, jnp.bfloat16

NX, NY, NZ = 4, 4, 8
GROUPS = NX * NZ
OTHER_CORE = [(i, i ^ 1) for i in range(2 * NY)]
STEPS = (1, 3, 2)
VMEM = 40 * 2**20


def call(body, name, out, *operands, grid=(), prefetch=(), ins=None, outs=None, scratch=(), flops=0, size=0):
    whole = pl.BlockSpec(memory_space=pltpu.VMEM)
    if ins is None:
        ins, outs = [whole] * len(operands), jax.tree.map(lambda _: whole, out)
    return pl.pallas_call(
        body,
        grid_spec=pltpu.PrefetchScalarGridSpec(
            num_scalar_prefetch=len(prefetch), grid=grid, in_specs=ins, out_specs=outs, scratch_shapes=scratch
        ),
        out_shape=out,
        cost_estimate=pl.CostEstimate(flops=flops, bytes_accessed=size, transcendentals=0),
        compiler_params=pltpu.CompilerParams(vmem_limit_bytes=VMEM),
        name=name,
    )(*prefetch, *operands)


def array(shape, dtype):
    return jax.ShapeDtypeStruct(shape, dtype)


def dot(a, b, over_a=1, over_b=0):
    return lax.dot_general(a, b, (((over_a,), (over_b,)), ((), ())), preferred_element_type=f32)


def own_slots(at_ref, count_ref):
    seq = at_ref[2]
    offset = lax.fori_loop(0, GROUPS, lambda g, o: o + jnp.where(g < seq, count_ref[g], 0), jnp.int32(0))
    return offset, count_ref[seq]


def sort_kernel(at_ref, count_ref, rows_ref, gain_ref, out_ref, inv_ref):
    vocab = at_ref[3]
    slots, features = rows_ref.shape
    turns, share = out_ref.shape[1:]
    offset, count = own_slots(at_ref, count_ref)
    square = jnp.zeros((slots, share), f32)
    for i in range(0, features, share):
        values = rows_ref[:, i : i + share].astype(f32)
        square += values * values
    inv_rms = lax.rsqrt(jnp.sum(square, axis=1, keepdims=True) / features + norm_eps)
    inv_ref[...] = jnp.broadcast_to(inv_rms, inv_ref.shape)
    part = pl.ds(pl.multiple_of(vocab * share, share), share)
    normed = (rows_ref[:, part].astype(f32) * inv_rms * gain_ref[:, part]).astype(bf16)
    to = lax.broadcasted_iota(jnp.int32, (slots, slots), 0)
    source = lax.broadcasted_iota(jnp.int32, (slots, slots), 1)
    kind = sum((to >= i * turns).astype(jnp.int32) for i in range(1, NX))
    row = ((kind - offset) & (NX - 1)) + NX * (to - kind * turns)
    pick = jnp.where((row == source) & (row < count), 1.0, 0.0).astype(bf16)
    by_class = dot(pick, normed).astype(bf16)
    for g in range(out_ref.shape[0]):
        k = g % NX
        out_ref[g] = by_class[k * turns : (k + 1) * turns]


def teacher_kernel(first_ref, index_ref, logprob_ref, dense_ref):
    local = index_ref[...] - first_ref[0]
    prob = jnp.exp(logprob_ref[...])
    width, tokens = dense_ref.shape
    step = 200
    for start in range(0, width, step):
        size = min(step, width - start)
        ids = lax.broadcasted_iota(jnp.int32, (size, tokens), 0) + start
        dense = jnp.zeros((size, tokens), f32)
        for j in range(local.shape[0]):
            dense = jnp.where(local[j : j + 1, :] == ids, prob[j : j + 1, :], dense)
        dense_ref[start : start + size, :] = dense


def teacher_columns(first_column, index, logprob, width):
    entries, tokens = index.shape
    block = 128
    return call(
        teacher_kernel, "teacher_columns", array((width, tokens), f32), index, logprob,
        grid=(tokens // block,), prefetch=(first_column.reshape(1),),
        ins=[pl.BlockSpec((entries, block), lambda i, s: (0, i))] * 2,
        outs=pl.BlockSpec((width, block), lambda i, s: (0, i)),
        flops=4 * tokens * width * entries, size=4 * tokens * width,
    )


def place_kernel(at_ref, *refs):
    x, y = at_ref[0], at_ref[1]
    by_x, by_y, (x_ref, y_ref) = refs[:4], refs[4:8], refs[8:]
    for k in range(4):
        x_ref[(x + k) % 4] = by_x[k][...]
        y_ref[(y + k) % 4] = by_y[k][...]


def gather_kernel(at_ref, *refs):
    x, y = at_ref[0], at_ref[1]
    by_y, by_x, out_ref = refs[:4], refs[4:8], refs[8]
    rows = by_x[0].shape[1]
    for k in range(4):
        out_ref[(y + k) % 4, 0] = by_y[k][...]
        start = pl.multiple_of((x + k) % 4 * rows, 64)
        for j in range(4):
            out_ref[j, 1, pl.ds(start, rows), :] = by_x[k][j]


def logits_part(rows_ref, weight_ref):
    half = rows_ref.shape[3]
    return dot(weight_ref[:, :half], rows_ref[0, 0], 1, 1) + dot(weight_ref[:, half:], rows_ref[0, 1], 1, 1)


def logits_own_kernel(block_ref, rows_ref, weight_ref, out_ref):
    part = logits_part(rows_ref, weight_ref)

    @pl.when(pl.program_id(0) == 0)
    def _():
        out_ref[...] = part

    @pl.when(pl.program_id(0) > 0)
    def _():
        out_ref[...] += part


def logits_rest_kernel(block_ref, rows_ref, weight_ref, own_ref, dense_ref, out_ref, stats_ref):
    part = logits_part(rows_ref, weight_ref)

    @pl.when(pl.program_id(0) == 0)
    def _():
        out_ref[...] = own_ref[...] + part

    @pl.when(pl.program_id(0) > 0)
    def _():
        out_ref[...] += part

    @pl.when(pl.program_id(0) == pl.num_programs(0) - 1)
    def _():
        tokens, step = out_ref.shape[1], 128
        for i in range(0, tokens, step):
            logits = out_ref[:, i : i + step]
            peak = jnp.max(logits, axis=0, keepdims=True)
            total = peak + jnp.log(jnp.sum(jnp.exp(logits - peak), axis=0, keepdims=True))
            stats_ref[:, i : i + step] = total
            stats_ref[:, tokens + i : tokens + i + step] = jnp.sum(
                logits * dense_ref[:, i : i + step], axis=0, keepdims=True
            )


def logits_call(blocks, rows, weight, own=None, dense=None):
    count, _, tokens, half = rows.shape
    width = weight.shape[0]
    whole = pl.BlockSpec((width, tokens), lambda k, b: (0, 0))
    ins = [
        pl.BlockSpec((1, 2, tokens, half), lambda k, b: (k, 0, 0, 0)),
        pl.BlockSpec((width, 2 * half), lambda k, b: (0, b[k])),
    ]
    options = dict(grid=(count,), prefetch=(blocks,), flops=4 * count * tokens * half * width, size=8 * 2**20)
    logits = array((width, tokens), f32)
    if own is None:
        return call(logits_own_kernel, "logits_own", logits, rows, weight, ins=ins, outs=whole, **options)
    return call(
        logits_rest_kernel, "logits_rest", [logits, array((1, 2 * tokens), f32)], rows, weight, own, dense,
        ins=[*ins, whole, whole], outs=[whole, pl.BlockSpec((1, 2 * tokens), lambda k, b: (0, 0))], **options,
    )


def grad_rest_kernel(
    block_ref, totals_ref, logits_ref, dense_ref, logprob_ref, weight_ref, grad_ref, turned_ref, out_ref, pad_ref
):
    width, tokens = logits_ref.shape

    @pl.when(pl.program_id(0) == 0)
    def _():
        step = pad_ref.shape[1]
        pad_ref[...] = jnp.zeros(pad_ref.shape, f32)
        for i in range(0, tokens, step):
            totals = totals_ref[:, i : i + step]
            peak = jnp.max(totals, axis=0, keepdims=True)
            total = peak + jnp.log(jnp.sum(jnp.exp(totals - peak), axis=0, keepdims=True))
            mass = jnp.sum(jnp.exp(logprob_ref[:, i : i + step]), axis=0, keepdims=True)
            student = mass * jnp.exp(logits_ref[:, i : i + step] - total)
            grad = loss_scale * (student - dense_ref[:, i : i + step])
            grad_ref[:, i : i + step] = grad.astype(bf16)
            pad_ref[:width, :] = grad
            turned_ref[i : i + step, :] = pad_ref[...].T[:, :width].astype(bf16)

    out = dot(turned_ref[...], weight_ref[...]).astype(bf16)
    half = out_ref.shape[3]
    out_ref[0, 0] = out[:, :half]
    out_ref[0, 1] = out[:, half:]


def grad_rest(blocks, totals, logits, dense, logprob, weight):
    width, tokens = logits.shape
    count = blocks.shape[0]
    half = weight.shape[1] // (4 * count)
    whole = pl.BlockSpec((width, tokens), lambda k, b: (0, 0))
    return call(
        grad_rest_kernel, "grad_rest",
        [array((width, tokens), bf16), array((tokens, width), bf16), array((count, 2, tokens, half), bf16)],
        totals, logits, dense, logprob, weight,
        grid=(count,), prefetch=(blocks,),
        ins=[
            pl.BlockSpec((totals.shape[0], tokens), lambda k, b: (0, 0)),
            whole,
            whole,
            pl.BlockSpec(logprob.shape, lambda k, b: (0, 0)),
            pl.BlockSpec((width, 2 * half), lambda k, b: (0, b[k])),
        ],
        outs=[
            whole,
            pl.BlockSpec((tokens, width), lambda k, b: (0, 0)),
            pl.BlockSpec((1, 2, tokens, half), lambda k, b: (k, 0, 0, 0)),
        ],
        scratch=[pltpu.VMEM((-(-width // 128) * 128, 128), f32)],
        flops=4 * count * tokens * half * width, size=12 * 2**20,
    )


def grad_own_kernel(block_ref, at_ref, turned_ref, weight_ref, other_ref, *refs):
    by_y, by_x, keep_ref = refs[:4], refs[4:8], refs[8]
    x, y = at_ref[0], at_ref[1]
    step = pl.program_id(0)
    out = dot(turned_ref[...], weight_ref[...])
    half = out.shape[1] // 2
    first = (out[:, :half] + other_ref[0, 0].astype(f32)).astype(bf16)
    for j in range(4):

        @pl.when(step == j)
        def _():
            by_y[j][...] = first

    second = (out[:, half:] + other_ref[0, 1].astype(f32)).astype(bf16)
    rows = keep_ref.shape[1]
    for k in range(4):
        keep_ref[k] = second[k * rows : (k + 1) * rows]
    for k in range(4):
        by_x[k][(y + step) % 4] = keep_ref[(x + k) % 4]


def grad_own(blocks, at, turned, weight, other):
    count, _, tokens, half = other.shape
    width = weight.shape[0]
    rows = tokens // NX
    piece, parts = pl.BlockSpec((tokens, half), lambda k, b, a: (0, 0)), pl.BlockSpec((NY, rows, half), lambda k, b, a: (0, 0, 0))
    return call(
        grad_own_kernel, "grad_own",
        [array((tokens, half), bf16)] * 4 + [array((NY, rows, half), bf16)] * 4,
        turned, weight, other,
        grid=(count,), prefetch=(blocks, at),
        ins=[
            pl.BlockSpec((tokens, width), lambda k, b, a: (0, 0)),
            pl.BlockSpec((width, 2 * half), lambda k, b, a: (0, b[k])),
            pl.BlockSpec((1, 2, tokens, half), lambda k, b, a: ((a[1] + k) % NY, 0, 0, 0)),
        ],
        outs=[piece] * 4 + [parts] * 4,
        scratch=[pltpu.VMEM((NX, rows, half), bf16)],
        flops=4 * count * tokens * half * width, size=12 * 2**20,
    )


def sum_kernel(at_ref, *refs):
    x, y = at_ref[0], at_ref[1]
    by_y, by_x, to_x, to_y, (keep_ref,) = refs[:4], refs[4:8], refs[8:12], refs[12:16], refs[16:]
    count, rows = by_x[0].shape[:2]
    for i in range(count):
        part = pl.ds(i * rows, rows)
        keep_ref[0, i] = sum(r[part, :].astype(f32) for r in by_y).astype(bf16)
        keep_ref[1, i] = sum(r[i].astype(f32) for r in by_x).astype(bf16)
    for k in range(4):
        to_x[k][...] = keep_ref[0, (x + k) % 4]
        to_y[k][...] = keep_ref[1, (y + k) % 4]


def spread_kernel(*refs):
    by_x, by_y, (spread_ref, target_ref, out_ref) = refs[:4], refs[4:8], refs[8:]
    both = jnp.concatenate(
        [sum(r[...].astype(f32) for r in by_x).astype(bf16), sum(r[...].astype(f32) for r in by_y).astype(bf16)], axis=1
    )
    turns, share = out_ref.shape[1] - 1, out_ref.shape[2]
    for z in range(spread_ref.shape[0]):
        rows = dot(spread_ref[z], both).astype(bf16)
        for k in range(NX):
            out_ref[z * NX + k, :turns, :] = rows[k * turns : (k + 1) * turns]
    rest = target_ref[...]
    step = rest.shape[2]
    for i in range(share // step):
        term = rest.astype(bf16)
        out_ref[:, turns:, i * step : (i + 1) * step] = term if i < 3 else jnp.zeros(term.shape, bf16)
        rest = rest - term.astype(f32)


def unsort_kernel(at_ref, count_ref, got_ref, rows_ref, gain_ref, u_ref, dots_ref, target_ref, sum_ref):
    offset, _ = own_slots(at_ref, count_ref)
    turns, share = sum_ref.shape[1:]
    lines = got_ref.shape[0] // NX
    target = jnp.zeros((1, share), f32)
    for k in range(NX):
        total = got_ref[k].astype(f32)
        for z in range(1, lines):
            total += got_ref[z * NX + k].astype(f32)
        sum_ref[k] = total[:turns]
        target += total[turns:]
    step = target_ref.shape[1]
    target_ref[...] = target[:, :step] + (target[:, step : 2 * step] + target[:, 2 * step : 3 * step])
    part = pl.ds(pl.multiple_of(at_ref[3] * share, share), share)
    for i in range(NX):
        for m in range(turns):
            u_ref[NX * m + i : NX * m + i + 1, :] = sum_ref[(offset + i) & (NX - 1), m : m + 1, :] * gain_ref[:, part]
    dots = jnp.sum(u_ref[...] * rows_ref[:, part].astype(f32), axis=1, keepdims=True)
    dots_ref[...] = jnp.broadcast_to(dots, dots_ref.shape)


def finish_kernel(at_ref, count_ref, *refs):
    parts, (u_ref, inv_ref, rows_ref, out_ref) = refs[:4], refs[4:]
    _, count = own_slots(at_ref, count_ref)
    dots = sum(r[:, :1] for r in parts)
    inv_rms = inv_ref[:, :1]
    share = out_ref.shape[1]
    part = pl.ds(pl.multiple_of(at_ref[3] * share, share), share)
    grad = (u_ref[...] - rows_ref[:, part].astype(f32) * (inv_rms * inv_rms * dots / rows_ref.shape[1])) * inv_rms
    live = lax.broadcasted_iota(jnp.int32, grad.shape, 0) < count
    out_ref[...] = jnp.where(live, grad, 0.0).astype(bf16)


def weight_grad_kernel(block_ref, own_ref, rest_ref, grad_ref, out_ref):
    def write(rows_ref):
        half = rows_ref.shape[3]
        for h in range(2):
            out_ref[:, h * half : (h + 1) * half] = dot(grad_ref[...], rows_ref[0, h]).astype(bf16)

    count = pl.num_programs(0) // 2

    @pl.when(pl.program_id(0) < count)
    def _():
        write(own_ref)

    @pl.when(pl.program_id(0) >= count)
    def _():
        write(rest_ref)


def weight_grad(blocks, own, rest, grad):
    count, _, tokens, half = own.shape
    width = grad.shape[0]
    return call(
        weight_grad_kernel, "weight_grad", array((width, 4 * count * half), bf16), own, rest, grad,
        grid=(2 * count,), prefetch=(blocks,),
        ins=[
            pl.BlockSpec((1, 2, tokens, half), lambda k, b: (jnp.minimum(k, count - 1), 0, 0, 0)),
            pl.BlockSpec((1, 2, tokens, half), lambda k, b: (jnp.maximum(k - count, 0), 0, 0, 0)),
            pl.BlockSpec((width, tokens), lambda k, b: (0, 0)),
        ],
        outs=pl.BlockSpec((width, 2 * half), lambda k, b: (0, b[k])),
        flops=8 * count * tokens * half * width, size=16 * 2**20,
    )


def exchange(x, axis):
    return lax.all_to_all(x, axis, 0, 0, tiled=True)


def along_x(x, k):
    return lax.ppermute(x, "seq", [(i, i // NX * NX + (i + k) % NX) for i in range(GROUPS)])


def along_y(x, k):
    return lax.ppermute(x, "vocab", [(i, (i + 2 * k) % (2 * NY)) for i in range(2 * NY)])


def from_ahead(x, move):
    got = {k: move(x, -k) for k in STEPS}
    return [x, got[1], got[2], got[3]]


def to_ahead(pieces, move):
    return [pieces[0], *(move(pieces[k], k) for k in STEPS)]


def merge(stats):
    tokens = stats[0].shape[1] // 2
    totals = [s[:, :tokens] for s in stats]
    peak = totals[0]
    for t in totals[1:]:
        peak = jnp.maximum(peak, t)
    total = peak + jnp.log(sum(jnp.exp(t - peak) for t in totals))
    return jnp.concatenate([total, sum(s[:, tokens:] for s in stats)], axis=1)


def per_device(rollout, group_count, final_gain, head_weight, teacher_index, teacher_logprob):
    slots, features = rollout.shape
    tokens, entries = teacher_index.shape
    width = head_weight.shape[1]
    weight = head_weight.T
    parts = 2 * NY
    share = features // parts
    half = share // 2
    class_rows = tokens // NX
    turns = slots // NX
    pack_rows = tokens // GROUPS
    seq = lax.axis_index("seq")
    own_z, own_x = seq // NX, seq % NX
    vocab = lax.axis_index("vocab")
    own_y, core = vocab // 2, vocab % 2
    at = jnp.stack([own_x, own_y, seq, vocab]).astype(jnp.int32)

    of_class, inv_rms = call(
        sort_kernel, "sort_rows", [array((GROUPS, turns, share), bf16), array((slots, 128), f32)],
        rollout, final_gain[None, :], prefetch=(at, group_count), size=2**19,
    )
    of_class = exchange(of_class, "seq")

    group_ids = jnp.arange(GROUPS, dtype=jnp.int32)
    before = group_ids[None, :] < group_ids[:, None]
    offsets = jnp.sum(jnp.where(before, group_count[None, :], 0), axis=1)
    turn_ids = jnp.arange(turns, dtype=jnp.int32)
    row_in_group = (own_x - offsets[:, None]) % NX + NX * turn_ids[None, :]
    rank = offsets[:, None] + row_in_group
    place = jnp.where(row_in_group < group_count[:, None], rank % GROUPS // NX * pack_rows + rank // GROUPS, class_rows)
    place_ids = jnp.arange(class_rows, dtype=jnp.int32)
    spread = (place.reshape(NZ, slots, 1) == place_ids[None, None, :]).astype(bf16)
    dense_rows = lax.dot_general(
        spread.reshape(-1, class_rows), of_class.reshape(-1, share), (((0,), (0,)), ((), ())), preferred_element_type=f32
    ).astype(bf16)

    by_x = from_ahead(dense_rows[:, :half], along_x)
    by_y = from_ahead(dense_rows[:, half:], along_y)
    all_x, all_y = call(
        place_kernel, "place", [array((4, class_rows, half), bf16)] * 2, *by_x, *by_y, prefetch=(at,), ins=None, size=2**21
    )
    by_y = from_ahead(all_x.reshape(tokens, half), along_y)
    by_x = from_ahead(all_y, along_x)

    def class_order(a):
        return a.reshape(NZ, NX, pack_rows, entries).transpose(1, 0, 2, 3).reshape(tokens, entries).T

    index = class_order(teacher_index)
    logprob = class_order(teacher_logprob)
    first_column = (seq * parts + vocab) * width
    dense = teacher_columns(first_column, index, logprob, width)
    by_y, by_x, dense = lax.optimization_barrier((by_y, by_x, dense))
    own_rows = call(
        gather_kernel, "gather_rows", array((NY, 2, tokens, half), bf16), *by_y, *by_x,
        prefetch=(at,), size=2**23,
    )
    rest_rows = lax.ppermute(own_rows, "vocab", OTHER_CORE)

    y_ids = jnp.arange(NY, dtype=jnp.int32)
    own_blocks = 2 * y_ids + core
    rest_blocks = 2 * y_ids + 1 - core
    logits_own = logits_call(own_blocks, own_rows, weight)
    logits, stats = logits_call(rest_blocks, rest_rows, weight, logits_own, dense)
    stats = merge([stats, lax.ppermute(stats, "vocab", OTHER_CORE)])
    stats = merge(from_ahead(stats, along_y))
    totals = exchange(jnp.broadcast_to(stats[:, :tokens], (GROUPS, tokens)), "seq")

    grad, turned, rest_grad = grad_rest(rest_blocks, totals, logits, dense, logprob, weight)
    other_grad = lax.ppermute(rest_grad, "vocab", OTHER_CORE)
    ahead_blocks = 2 * ((own_y + y_ids) % NY) + core
    pieces = grad_own(ahead_blocks, at, turned, weight, other_grad)
    by_y, by_x = to_ahead(pieces[:4], along_y), to_ahead(pieces[4:], along_x)
    weight_t = weight_grad(jnp.concatenate([own_blocks, rest_blocks]), own_rows, rest_rows, grad)

    own_tokens = own_x * class_rows + own_z * pack_rows
    totals = lax.dynamic_slice_in_dim(totals, own_tokens, pack_rows, 1)
    own_logprob = lax.dynamic_slice_in_dim(logprob, own_tokens, pack_rows, 1)
    peak = jnp.max(totals, axis=0)
    log_total = peak + jnp.log(jnp.sum(jnp.exp(totals - peak), axis=0))
    prob = jnp.exp(own_logprob)
    kl = jnp.sum(prob * own_logprob, axis=0) + jnp.sum(prob, axis=0) * log_total
    target = stats[0, tokens:].reshape(NX, NZ, pack_rows).transpose(1, 0, 2).reshape(GROUPS, 1, pack_rows)
    target = jnp.pad(target, ((0, 0), (0, 0), (0, 128 - pack_rows)))

    by_y, by_x, weight_t, kl, target = lax.optimization_barrier((by_y, by_x, weight_t, kl, target))
    small = array((class_rows, half), bf16)
    pieces = call(
        sum_kernel, "add_pieces", [small] * 8, *by_y, *by_x, prefetch=(at,),
        ins=[pl.BlockSpec(memory_space=pltpu.VMEM)] * 8, outs=[pl.BlockSpec(memory_space=pltpu.VMEM)] * 8,
        scratch=[pltpu.VMEM((2, 4, class_rows, half), bf16)], size=2**22,
    )
    by_x, by_y = to_ahead(pieces[:4], along_x), to_ahead(pieces[4:], along_y)
    spread_grad = call(
        spread_kernel, "spread_rows", array((GROUPS, turns + 1, share), bf16), *by_x, *by_y, spread, target, size=2**20
    )
    got = exchange(spread_grad, "seq")
    u, dots, targets = call(
        unsort_kernel, "unsort_rows",
        [array((slots, share), f32), array((slots, 128), f32), array((1, 128), f32)],
        got, rollout, final_gain[None, :], prefetch=(at, group_count),
        scratch=[pltpu.VMEM((NX, turns, share), f32)], size=2**19,
    )
    kl = kl - targets[0, :pack_rows]
    dots = dots + lax.ppermute(dots, "vocab", OTHER_CORE)
    grad_rollout = call(
        finish_kernel, "finish", array((slots, share), bf16), *from_ahead(dots, along_y), u, inv_rms, rollout,
        prefetch=(at, group_count), size=2**19,
    )
    return (kl, weight_t.T, grad_rollout)


def solution(mesh):
    placed = (P("seq", None), P(), P(), P(None, ("seq", "vocab")), P(), P())
    return jax.shard_map(
        per_device,
        mesh=mesh,
        in_specs=placed,
        out_specs=(P("seq"), P(None, ("seq", "vocab")), P("seq", "vocab")),
        check_vma=False,
    )
```

```python
import functools

import jax
import jax.numpy as jnp
from jax import lax
from jax.experimental import pallas as pl
from jax.experimental.pallas import tpu as pltpu
from jax.sharding import PartitionSpec as P

norm_eps = 1e-06
loss_scale = 16.0
f32, bf16 = jnp.float32, jnp.bfloat16

NX, NY, NZ = 4, 4, 8
GROUPS = NX * NZ
Y_LINES = [[y * 2 + core for y in range(NY)] for core in range(2)]
OTHER_CORE = [(i, i ^ 1) for i in range(2 * NY)]
STEPS = (1, 3, 2)
VMEM = 24 * 2**20


def call(body, name, out, *operands, grid=(), prefetch=(), ins=None, outs=None, scratch=(), flops=0, size=0):
    whole = pl.BlockSpec(memory_space=pltpu.VMEM)
    if ins is None:
        ins, outs = [whole] * len(operands), jax.tree.map(lambda _: whole, out)
    return pl.pallas_call(
        body,
        grid_spec=pltpu.PrefetchScalarGridSpec(
            num_scalar_prefetch=len(prefetch), grid=grid, in_specs=ins, out_specs=outs, scratch_shapes=scratch
        ),
        out_shape=out,
        cost_estimate=pl.CostEstimate(flops=flops, bytes_accessed=size, transcendentals=0),
        compiler_params=pltpu.CompilerParams(vmem_limit_bytes=VMEM),
        name=name,
    )(*prefetch, *operands)


def array(shape, dtype):
    return jax.ShapeDtypeStruct(shape, dtype)


def dot(a, b, over_a=1, over_b=0):
    return lax.dot_general(a, b, (((over_a,), (over_b,)), ((), ())), preferred_element_type=f32)


def own_slots(at_ref):
    seq = at_ref[2]
    offset = lax.fori_loop(0, GROUPS, lambda g, o: o + jnp.where(g < seq, at_ref[4 + g], 0), jnp.int32(0))
    return offset, at_ref[4 + seq]


def inverse_rms(rows_ref, step):
    slots, features = rows_ref.shape
    square = jnp.zeros((slots, step), f32)
    for i in range(0, features, step):
        values = rows_ref[:, i : i + step].astype(f32)
        square += values * values
    return lax.rsqrt(jnp.sum(square, axis=1, keepdims=True) / features + norm_eps)


def sort_kernel(at_ref, rows_ref, gain_ref, out_ref):
    vocab = at_ref[3]
    slots, features = rows_ref.shape
    turns, share = out_ref.shape[1:]
    offset, count = own_slots(at_ref)
    inv_rms = inverse_rms(rows_ref, share)
    part = pl.ds(pl.multiple_of(vocab * share, share), share)
    normed = (rows_ref[:, part].astype(f32) * inv_rms * gain_ref[:, part]).astype(bf16)
    to = lax.broadcasted_iota(jnp.int32, (slots, slots), 0)
    source = lax.broadcasted_iota(jnp.int32, (slots, slots), 1)
    kind = sum((to >= i * turns).astype(jnp.int32) for i in range(1, NX))
    row = ((kind - offset) & (NX - 1)) + NX * (to - kind * turns)
    pick = jnp.where((row == source) & (row < count), 1.0, 0.0).astype(bf16)
    by_class = dot(pick, normed).astype(bf16)
    for g in range(out_ref.shape[0]):
        k = g % NX
        out_ref[g] = by_class[k * turns : (k + 1) * turns]


def teacher_kernel(first_ref, index_ref, logprob_ref, dense_ref):
    local = index_ref[...] - first_ref[0]
    prob = jnp.exp(logprob_ref[...])
    width, tokens = dense_ref.shape
    step = 200
    for start in range(0, width, step):
        size = min(step, width - start)
        ids = lax.broadcasted_iota(jnp.int32, (size, tokens), 0) + start
        dense = jnp.zeros((size, tokens), f32)
        for j in range(local.shape[0]):
            dense = jnp.where(local[j : j + 1, :] == ids, prob[j : j + 1, :], dense)
        dense_ref[start : start + size, :] = dense


def teacher_columns(first_column, index, logprob, width):
    entries, tokens = index.shape
    block = 128
    return call(
        teacher_kernel, "teacher_columns", array((width, tokens), f32), index, logprob,
        grid=(tokens // block,), prefetch=(first_column.reshape(1),),
        ins=[pl.BlockSpec((entries, block), lambda i, s: (0, i))] * 2,
        outs=pl.BlockSpec((width, block), lambda i, s: (0, i)),
        flops=4 * tokens * width * entries, size=4 * tokens * width,
    )


def place_kernel(at_ref, *refs):
    by_x, out_ref = refs[:4], refs[4]
    for k in range(4):
        piece = by_x[k][...]
        for y in range(4):
            out_ref[y, (at_ref[0] + k) % 4] = piece


def gather_kernel(at_ref, *refs):
    by_x, out_ref = refs[:4], refs[4]
    for k in range(4):
        for y in range(4):
            out_ref[y, (at_ref[0] + k) % 4] = by_x[k][y]


def columns(weight_ref, blocks_ref, start, size):
    width = weight_ref.shape[1] // (2 * NY)
    parts = [pl.ds(pl.multiple_of(blocks_ref[k] * width + start, 256), size) for k in range(NY)]
    return jnp.concatenate([weight_ref[:, p] for p in parts], axis=1)


def side_by_side(rows_ref, part):
    return jnp.concatenate([rows_ref[k, part, :] for k in range(rows_ref.shape[0])], axis=1)


def half_logits_kernel(block_ref, rows_ref, weight_ref, *refs, second, step):
    out_ref = refs[-1]
    half = rows_ref.shape[2]
    left = columns(weight_ref, block_ref, second * half, half)
    for i in range(0, out_ref.shape[1], step):
        part = dot(left, side_by_side(rows_ref, pl.ds(i, step)), 1, 1)
        out_ref[:, i : i + step] = part if len(refs) == 1 else refs[0][:, i : i + step] + part


def half_logits(blocks, second, rows, weight, *before):
    count, tokens, half = rows.shape
    width = weight.shape[0]
    body = functools.partial(half_logits_kernel, second=second, step=256)
    return call(
        body, "logits_half", array((width, tokens), f32), rows, weight, *before,
        prefetch=(blocks,), flops=2 * count * tokens * half * width, size=6 * 2**20,
    )


def logits_rest_kernel(block_ref, first_ref, second_ref, weight_ref, own_ref, dense_ref, out_ref, stats_ref, *, step):
    tokens, half = out_ref.shape[1], first_ref.shape[2]
    left = jnp.concatenate([columns(weight_ref, block_ref, h * half, half) for h in range(2)], axis=1)
    for i in range(0, tokens, step):
        here = pl.ds(i, step)
        right = jnp.concatenate([side_by_side(first_ref, here), side_by_side(second_ref, here)], axis=1)
        logits = own_ref[:, i : i + step] + dot(left, right, 1, 1)
        out_ref[:, i : i + step] = logits
        peak = jnp.max(logits, axis=0, keepdims=True)
        weights = jnp.exp(logits - peak)
        total = jnp.sum(weights, axis=0, keepdims=True)
        stats_ref[:, i : i + step] = peak + jnp.log(total)
        target = jnp.sum(logits * dense_ref[:, i : i + step], axis=0, keepdims=True)
        stats_ref[:, tokens + i : tokens + i + step] = target
        mean = jnp.sum(weights * logits, axis=0, keepdims=True) / total
        stats_ref[:, 2 * tokens + i : 2 * tokens + i + step] = mean


def logits_call(blocks, rows, weight, own, dense):
    count, tokens, half = rows[0].shape
    width = weight.shape[0]
    return call(
        functools.partial(logits_rest_kernel, step=256), "logits_rest",
        [array((width, tokens), f32), array((1, 3 * tokens), f32)], *rows, weight, own, dense,
        prefetch=(blocks,), flops=4 * count * tokens * half * width, size=8 * 2**20,
    )


def grad_kernel(
    block_ref, stats_ref, logits_ref, dense_ref, logprob_ref, weight_ref, grad_ref, turned_ref, out_ref, pad_ref
):
    width, tokens = logits_ref.shape
    step = pad_ref.shape[1]
    pad_ref[...] = jnp.zeros(pad_ref.shape, f32)
    for i in range(0, tokens, step):
        totals = stats_ref[:, i : i + step]
        peak = jnp.max(totals, axis=0, keepdims=True)
        total = peak + jnp.log(jnp.sum(jnp.exp(totals - peak), axis=0, keepdims=True))
        mass = jnp.sum(jnp.exp(logprob_ref[:, i : i + step]), axis=0, keepdims=True)
        student = mass * jnp.exp(logits_ref[:, i : i + step] - total)
        grad = loss_scale * (student - dense_ref[:, i : i + step])
        grad_ref[:, i : i + step] = grad.astype(bf16)
        pad_ref[:width, :] = grad
        turned_ref[i : i + step, :] = pad_ref[...].T[:, :width].astype(bf16)
    rest_kernel(block_ref, turned_ref, weight_ref, out_ref, second=0)


def feature_part(weight_ref, blocks_ref, k, second):
    half = weight_ref.shape[1] // (4 * NY)
    return weight_ref[:, pl.ds(pl.multiple_of(blocks_ref[k] * 2 * half + second * half, 256), half)]


def grad_call(blocks, stats, logits, dense, logprob, weight):
    width, tokens = logits.shape
    count = blocks.shape[0]
    half = weight.shape[1] // (4 * count)
    inside = pl.BlockSpec(memory_space=pltpu.VMEM)
    return call(
        grad_kernel, "grad_logits",
        [array((width, tokens), bf16), array((tokens, width), bf16), array((count, tokens, half), bf16)],
        stats, logits, dense, logprob, weight, prefetch=(blocks,), ins=[inside] * 5, outs=[inside] * 3,
        scratch=[pltpu.VMEM((-(-width // 128) * 128, 128), f32)],
        flops=2 * count * tokens * half * width, size=12 * 2**20,
    )


def rest_kernel(block_ref, turned_ref, weight_ref, out_ref, *, second):
    for k in range(out_ref.shape[0]):
        out_ref[k] = dot(turned_ref[...], feature_part(weight_ref, block_ref, k, second)).astype(bf16)


def add_kernel(block_ref, turned_ref, weight_ref, other_ref, out_ref, *, second):
    for k in range(out_ref.shape[0]):
        out = dot(turned_ref[...], feature_part(weight_ref, block_ref, k, second))
        out_ref[k] = (out + other_ref[k].astype(f32)).astype(bf16)


def split_kernel(block_ref, at_ref, turned_ref, weight_ref, other_ref, *refs, second):
    by_x, keep_ref = refs[:4], refs[4]
    rows = keep_ref.shape[2]
    for y in range(other_ref.shape[0]):
        out = dot(turned_ref[...], feature_part(weight_ref, block_ref, y, second))
        out = (out + other_ref[y].astype(f32)).astype(bf16)
        for k in range(4):
            keep_ref[k, y] = out[k * rows : (k + 1) * rows]
    for k in range(4):
        by_x[k][...] = keep_ref[(at_ref[0] + k) % 4]


def half_call(body, name, blocks, second, turned, weight, *other, at=None):
    tokens, width = turned.shape
    count = blocks.shape[0]
    half = weight.shape[1] // (4 * count)
    rows = tokens // NX
    inside = pl.BlockSpec(memory_space=pltpu.VMEM)
    if at is None:
        out, outs, scratch, prefetch = array((count, tokens, half), bf16), inside, (), (blocks,)
    else:
        out, outs = [array((count, rows, half), bf16)] * 4, [inside] * 4
        scratch, prefetch = [pltpu.VMEM((NX, count, rows, half), bf16)], (blocks, at)
    return call(
        functools.partial(body, second=second), name, out, turned, weight, *other, prefetch=prefetch, scratch=scratch,
        ins=[inside] * (2 + len(other)), outs=outs, flops=2 * count * tokens * half * width, size=6 * 2**20,
    )


def sum_kernel(at_ref, by_y_ref, *refs):
    by_x, to_x, to_y_ref, keep_ref = refs[:4], refs[4:8], refs[8], refs[9]
    count, rows = by_x[0].shape[:2]
    for i in range(count):
        part = pl.ds(i * rows, rows)
        keep_ref[i] = sum(by_y_ref[j, part, :].astype(f32) for j in range(count)).astype(bf16)
        to_y_ref[i] = sum(r[i].astype(f32) for r in by_x).astype(bf16)
    for k in range(4):
        to_x[k][...] = keep_ref[(at_ref[0] + k) % 4]


def tokens_kernel(stats_ref, logprob_ref, kl_ref, dots_ref):
    tokens = kl_ref.shape[1]
    logprob = logprob_ref[...]
    prob = jnp.exp(logprob)
    mass = jnp.sum(prob, axis=0, keepdims=True)
    totals = stats_ref[:, :tokens]
    peak = jnp.max(totals, axis=0, keepdims=True)
    weights = jnp.exp(totals - peak)
    total = jnp.sum(weights, axis=0, keepdims=True)
    target = jnp.sum(stats_ref[:, tokens : 2 * tokens], axis=0, keepdims=True)
    mean = jnp.sum(weights * stats_ref[:, 2 * tokens :], axis=0, keepdims=True) / total
    kl_ref[...] = jnp.sum(prob * logprob, axis=0, keepdims=True) - target + mass * (peak + jnp.log(total))
    dots_ref[...] = loss_scale * (mass * mean - target)


def spread_kernel(*refs):
    by_x, (by_y_ref, spread_ref, out_ref) = refs[:4], refs[4:]
    first = sum(r[...].astype(f32) for r in by_x)
    second = sum(by_y_ref[j].astype(f32) for j in range(by_y_ref.shape[0]))
    both = jnp.concatenate([first.astype(bf16), second.astype(bf16)], axis=1)
    turns = out_ref.shape[1]
    slots = NX * turns
    for z in range(out_ref.shape[0] // NX):
        rows = dot(spread_ref[z * slots : (z + 1) * slots, :].astype(bf16), both).astype(bf16)
        for k in range(NX):
            out_ref[z * NX + k] = rows[k * turns : (k + 1) * turns]


def finish_kernel(at_ref, got_ref, rows_ref, gain_ref, dots_ref, out_ref, sum_ref, grad_ref):
    offset, count = own_slots(at_ref)
    turns, share = sum_ref.shape[1:]
    slots, features = rows_ref.shape
    tokens = dots_ref.shape[1]
    for k in range(NX):
        total = got_ref[k].astype(f32)
        for z in range(1, got_ref.shape[0] // NX):
            total += got_ref[z * NX + k].astype(f32)
        sum_ref[k] = total
    for i in range(NX):
        for m in range(turns):
            grad_ref[NX * m + i : NX * m + i + 1, :] = sum_ref[(offset + i) & (NX - 1), m : m + 1, :]
    rank = offset + lax.broadcasted_iota(jnp.int32, (slots, tokens), 0)
    row = (rank & (NX - 1)) * (tokens // NX) + ((rank & (GROUPS - 1)) >> 2) * (tokens // GROUPS) + (rank >> 5)
    here = row == lax.broadcasted_iota(jnp.int32, (slots, tokens), 1)
    dots = jnp.sum(jnp.where(here, dots_ref[...], 0.0), axis=1, keepdims=True)
    part = pl.ds(pl.multiple_of(at_ref[3] * share, share), share)
    inv_rms = inverse_rms(rows_ref, share)
    grad = (grad_ref[...] * gain_ref[:, part] - rows_ref[:, part].astype(f32) * (inv_rms * dots / features)) * inv_rms
    live = lax.broadcasted_iota(jnp.int32, grad.shape, 0) < count
    out_ref[...] = jnp.where(live, grad, 0.0).astype(bf16)


def weight_grad_kernel(block_ref, *refs):
    own, rest, grad_ref, out_ref = refs[:2], refs[2:4], refs[4], refs[5]

    def write(rows):
        half = rows[0].shape[2]
        for h in range(2):
            out_ref[:, h * half : (h + 1) * half] = dot(grad_ref[...], rows[h][0]).astype(bf16)

    count = pl.num_programs(0) // 2

    @pl.when(pl.program_id(0) < count)
    def _():
        write(own)

    @pl.when(pl.program_id(0) >= count)
    def _():
        write(rest)


def weight_grad(blocks, own, rest, grad):
    count, tokens, half = own[0].shape
    width = grad.shape[0]
    return call(
        weight_grad_kernel, "weight_grad", array((width, 4 * count * half), bf16), *own, *rest, grad,
        grid=(2 * count,), prefetch=(blocks,),
        ins=[
            *[pl.BlockSpec((1, tokens, half), lambda k, b: (jnp.minimum(k, count - 1), 0, 0))] * 2,
            *[pl.BlockSpec((1, tokens, half), lambda k, b: (jnp.maximum(k - count, 0), 0, 0))] * 2,
            pl.BlockSpec((width, tokens), lambda k, b: (0, 0)),
        ],
        outs=pl.BlockSpec((width, 2 * half), lambda k, b: (0, b[k])),
        flops=8 * count * tokens * half * width, size=16 * 2**20,
    )


def after(small, *others):
    return lax.optimization_barrier((small, others))[0]


def exchange(x, axis, lines=None):
    return lax.all_to_all(x, axis, 0, 0, tiled=True, axis_index_groups=lines)


def along_x(x, k):
    return lax.ppermute(x, "seq", [(i, i // NX * NX + (i + k) % NX) for i in range(GROUPS)])


def along_y(x, k):
    return lax.ppermute(x, "vocab", [(i, (i + 2 * k) % (2 * NY)) for i in range(2 * NY)])


def from_ahead(x, move):
    got = {k: move(x, -k) for k in STEPS}
    return [x, got[1], got[2], got[3]]


def to_ahead(pieces, move):
    return [pieces[0], *(move(pieces[k], k) for k in STEPS)]


def merge(stats):
    tokens = stats[0].shape[1] // 3
    totals = [s[:, :tokens] for s in stats]
    peak = totals[0]
    for t in totals[1:]:
        peak = jnp.maximum(peak, t)
    weights = [jnp.exp(t - peak) for t in totals]
    total = sum(weights)
    target = sum(s[:, tokens : 2 * tokens] for s in stats)
    mean = sum(w * s[:, 2 * tokens :] for w, s in zip(weights, stats)) / total
    return jnp.concatenate([peak + jnp.log(total), target, mean], axis=1)


def per_device(rollout, group_count, final_gain, head_weight, teacher_index, teacher_logprob):
    slots, features = rollout.shape
    tokens, entries = teacher_index.shape
    width = head_weight.shape[1]
    weight = head_weight.T
    parts = 2 * NY
    share = features // parts
    half = share // 2
    class_rows = tokens // NX
    turns = slots // NX
    pack_rows = tokens // GROUPS
    seq = lax.axis_index("seq")
    own_z, own_x = seq // NX, seq % NX
    vocab = lax.axis_index("vocab")
    own_y, core = vocab // 2, vocab % 2
    at = jnp.concatenate([jnp.stack([own_x, own_y, seq, vocab]).astype(jnp.int32), group_count])

    of_class = call(
        sort_kernel, "sort_rows", array((GROUPS, turns, share), bf16), rollout, final_gain[None, :], prefetch=(at,), size=2**19
    )
    of_class = exchange(of_class, "seq")

    def class_order(a):
        return a.reshape(NZ, NX, pack_rows, entries).transpose(1, 0, 2, 3).reshape(tokens, entries).T

    index = class_order(teacher_index)
    logprob = class_order(teacher_logprob)
    first_column = (seq * parts + vocab) * width
    dense = teacher_columns(first_column, index, logprob, width)

    group_ids = jnp.arange(GROUPS, dtype=jnp.int32)
    before = group_ids[None, :] < group_ids[:, None]
    offsets = jnp.sum(jnp.where(before, group_count[None, :], 0), axis=1)
    turn_ids = jnp.arange(turns, dtype=jnp.int32)
    row_in_group = (own_x - offsets[:, None]) % NX + NX * turn_ids[None, :]
    rank = offsets[:, None] + row_in_group
    place = jnp.where(row_in_group < group_count[:, None], rank % GROUPS // NX * pack_rows + rank // GROUPS, class_rows)
    place_ids = jnp.arange(class_rows, dtype=jnp.int32)
    place = after(place, dense)
    spread = lax.optimization_barrier((place.reshape(-1, 1) == place_ids[None, :]).astype(f32))
    dense_rows = dot(spread.astype(bf16), of_class.reshape(-1, share), 0, 0).astype(bf16)

    by_x = from_ahead(dense_rows[:, :half], along_x)
    all_y = exchange(jnp.broadcast_to(dense_rows[:, half:], (NY, class_rows, half)), "vocab", Y_LINES)
    all_x = call(place_kernel, "place", array((NY, NX, class_rows, half), bf16), *by_x, prefetch=(at,), size=2**21)
    by_x = from_ahead(all_y, along_x)
    own_first = exchange(all_x.reshape(NY, tokens, half), "vocab", Y_LINES)

    y_ids = jnp.arange(NY, dtype=jnp.int32)
    own_blocks = 2 * y_ids + core
    rest_blocks = 2 * y_ids + 1 - core
    own_second = call(
        gather_kernel, "gather_rows", array((NY, NX, class_rows, half), bf16), *by_x, prefetch=(at,), size=2**22
    ).reshape(NY, tokens, half)
    rest_second = lax.ppermute(own_second, "vocab", OTHER_CORE)
    logits_own = half_logits(own_blocks, 1, own_second, weight)
    rest_first = lax.ppermute(own_first, "vocab", OTHER_CORE)
    logits_own = half_logits(after(own_blocks, logits_own), 0, own_first, weight, logits_own)
    own_rows, rest_rows = [own_first, own_second], [rest_first, rest_second]
    logits, stats = logits_call(rest_blocks, rest_rows, weight, logits_own, dense)
    stats = merge([stats, lax.ppermute(stats, "vocab", OTHER_CORE)])
    stats = merge(from_ahead(stats, along_y))
    stats = exchange(jnp.broadcast_to(stats, (GROUPS, 3 * tokens)), "seq")

    grad, turned, rest_first = grad_call(rest_blocks, stats, logits, dense, logprob, weight)
    other_first = lax.ppermute(rest_first, "vocab", OTHER_CORE)
    other_second = lax.ppermute(half_call(rest_kernel, "grad_rest", rest_blocks, 1, turned, weight), "vocab", OTHER_CORE)
    first = half_call(add_kernel, "grad_first", own_blocks, 0, turned, weight, other_first)
    by_y = exchange(first, "vocab", Y_LINES)
    pieces = half_call(split_kernel, "grad_second", after(own_blocks, first), 1, turned, weight, other_second, at=at)
    by_x = to_ahead(pieces, along_x)
    weight_t = weight_grad(after(jnp.concatenate([own_blocks, rest_blocks]), pieces), own_rows, rest_rows, grad)
    kl, dots = call(tokens_kernel, "tokens", [array((1, tokens), f32)] * 2, stats, logprob, size=2**19)
    kl = lax.dynamic_slice_in_dim(kl[0], own_x * class_rows + own_z * pack_rows, pack_rows)
    at = after(at, weight_t, kl, dots)

    small = array((class_rows, half), bf16)
    inside = pl.BlockSpec(memory_space=pltpu.VMEM)
    *pieces, to_y = call(
        sum_kernel, "add_pieces", [small] * 4 + [array((NY, class_rows, half), bf16)], by_y, *by_x, prefetch=(at,),
        ins=[inside] * 5, outs=[inside] * 5, scratch=[pltpu.VMEM((NX, class_rows, half), bf16)], size=2**22,
    )
    by_x = to_ahead(pieces, along_x)
    by_y = exchange(to_y, "vocab", Y_LINES)
    spread_grad = call(
        spread_kernel, "spread_rows", array((GROUPS, turns, share), bf16), *by_x, by_y, spread, size=2**20
    )
    grad_rollout = call(
        finish_kernel, "finish", array((slots, share), bf16), exchange(spread_grad, "seq"), rollout, final_gain[None, :],
        dots, prefetch=(at,), ins=[inside] * 4, outs=inside,
        scratch=[pltpu.VMEM((NX, turns, share), f32), pltpu.VMEM((slots, share), f32)], size=2**19,
    )
    return (kl, weight_t.T, grad_rollout)


def solution(mesh):
    placed = (P("seq", None), P(), P(), P(None, ("seq", "vocab")), P(), P())
    return jax.shard_map(
        per_device,
        mesh=mesh,
        in_specs=placed,
        out_specs=(P("seq"), P(None, ("seq", "vocab")), P("seq", "vocab")),
        check_vma=False,
    )
```

```python
import functools

import jax
import jax.numpy as jnp
from jax import lax
from jax.experimental import pallas as pl
from jax.experimental.pallas import tpu as pltpu
from jax.sharding import PartitionSpec as P

norm_eps = 1e-06
loss_scale = 16.0
f32, bf16 = jnp.float32, jnp.bfloat16

NX, NY, NZ = 4, 4, 8
GROUPS = NX * NZ
Y_LINES = [[y * 2 + core for y in range(NY)] for core in range(2)]
OTHER_CORE = [(i, i ^ 1) for i in range(2 * NY)]
STEPS = (1, 3, 2)
VMEM = 24 * 2**20


def call(body, name, out, *operands, grid=(), prefetch=(), ins=None, outs=None, scratch=(), flops=0, size=0):
    whole = pl.BlockSpec(memory_space=pltpu.VMEM)
    if ins is None:
        ins, outs = [whole] * len(operands), jax.tree.map(lambda _: whole, out)
    return pl.pallas_call(
        body,
        grid_spec=pltpu.PrefetchScalarGridSpec(
            num_scalar_prefetch=len(prefetch), grid=grid, in_specs=ins, out_specs=outs, scratch_shapes=scratch
        ),
        out_shape=out,
        cost_estimate=pl.CostEstimate(flops=flops, bytes_accessed=size, transcendentals=0),
        compiler_params=pltpu.CompilerParams(vmem_limit_bytes=VMEM),
        name=name,
    )(*prefetch, *operands)


def array(shape, dtype):
    return jax.ShapeDtypeStruct(shape, dtype)


def dot(a, b, over_a=1, over_b=0):
    return lax.dot_general(a, b, (((over_a,), (over_b,)), ((), ())), preferred_element_type=f32)


def own_slots(at_ref):
    seq = at_ref[2]
    offset = lax.fori_loop(0, GROUPS, lambda g, o: o + jnp.where(g < seq, at_ref[4 + g], 0), jnp.int32(0))
    return offset, at_ref[4 + seq]


def inverse_rms(rows_ref, step):
    slots, features = rows_ref.shape
    square = jnp.zeros((slots, step), f32)
    for i in range(0, features, step):
        values = rows_ref[:, i : i + step].astype(f32)
        square += values * values
    return lax.rsqrt(jnp.sum(square, axis=1, keepdims=True) / features + norm_eps)


def sort_kernel(at_ref, rows_ref, gain_ref, out_ref):
    vocab = at_ref[3]
    slots, features = rows_ref.shape
    turns, share = out_ref.shape[1:]
    offset, count = own_slots(at_ref)
    inv_rms = inverse_rms(rows_ref, share)
    part = pl.ds(pl.multiple_of(vocab * share, share), share)
    normed = (rows_ref[:, part].astype(f32) * inv_rms * gain_ref[:, part]).astype(bf16)
    to = lax.broadcasted_iota(jnp.int32, (slots, slots), 0)
    source = lax.broadcasted_iota(jnp.int32, (slots, slots), 1)
    kind = sum((to >= i * turns).astype(jnp.int32) for i in range(1, NX))
    row = ((kind - offset) & (NX - 1)) + NX * (to - kind * turns)
    pick = jnp.where((row == source) & (row < count), 1.0, 0.0).astype(bf16)
    by_class = dot(pick, normed).astype(bf16)
    for g in range(out_ref.shape[0]):
        k = g % NX
        out_ref[g] = by_class[k * turns : (k + 1) * turns]


def teacher_kernel(first_ref, index_ref, logprob_ref, dense_ref):
    local = index_ref[...] - first_ref[0]
    prob = jnp.exp(logprob_ref[...])
    width, tokens = dense_ref.shape
    step = 200
    for start in range(0, width, step):
        size = min(step, width - start)
        ids = lax.broadcasted_iota(jnp.int32, (size, tokens), 0) + start
        dense = jnp.zeros((size, tokens), f32)
        for j in range(local.shape[0]):
            dense = jnp.where(local[j : j + 1, :] == ids, prob[j : j + 1, :], dense)
        dense_ref[start : start + size, :] = dense


def teacher_columns(first_column, index, logprob, width):
    entries, tokens = index.shape
    block = 128
    return call(
        teacher_kernel, "teacher_columns", array((width, tokens), f32), index, logprob,
        grid=(tokens // block,), prefetch=(first_column.reshape(1),),
        ins=[pl.BlockSpec((entries, block), lambda i, s: (0, i))] * 2,
        outs=pl.BlockSpec((width, block), lambda i, s: (0, i)),
        flops=4 * tokens * width * entries, size=4 * tokens * width,
    )


def place_kernel(at_ref, *refs):
    by_x, out_ref = refs[:4], refs[4]
    for k in range(4):
        piece = by_x[k][...]
        for y in range(4):
            out_ref[y, (at_ref[0] + k) % 4] = piece


def gather_kernel(at_ref, *refs):
    by_x, out_ref = refs[:4], refs[4]
    for k in range(4):
        for y in range(4):
            out_ref[y, (at_ref[0] + k) % 4] = by_x[k][y]


def columns(weight_ref, blocks_ref, start, size):
    width = weight_ref.shape[1] // (2 * NY)
    parts = [pl.ds(pl.multiple_of(blocks_ref[k] * width + start, 256), size) for k in range(NY)]
    return jnp.concatenate([weight_ref[:, p] for p in parts], axis=1)


def side_by_side(rows_ref, part):
    return jnp.concatenate([rows_ref[k, part, :] for k in range(rows_ref.shape[0])], axis=1)


def half_logits_kernel(block_ref, rows_ref, weight_ref, *refs, second, step):
    out_ref = refs[-1]
    half = rows_ref.shape[2]
    left = columns(weight_ref, block_ref, second * half, half)
    for i in range(0, out_ref.shape[1], step):
        part = dot(left, side_by_side(rows_ref, pl.ds(i, step)), 1, 1)
        out_ref[:, i : i + step] = part if len(refs) == 1 else refs[0][:, i : i + step] + part


def half_logits(blocks, second, rows, weight, *before):
    count, tokens, half = rows.shape
    width = weight.shape[0]
    body = functools.partial(half_logits_kernel, second=second, step=256)
    return call(
        body, "logits_half", array((width, tokens), f32), rows, weight, *before,
        prefetch=(blocks,), flops=2 * count * tokens * half * width, size=6 * 2**20,
    )


def logits_rest_kernel(block_ref, first_ref, second_ref, weight_ref, own_ref, dense_ref, out_ref, stats_ref, *, step):
    tokens, half = out_ref.shape[1], first_ref.shape[2]
    left = jnp.concatenate([columns(weight_ref, block_ref, h * half, half) for h in range(2)], axis=1)
    for i in range(0, tokens, step):
        here = pl.ds(i, step)
        right = jnp.concatenate([side_by_side(first_ref, here), side_by_side(second_ref, here)], axis=1)
        logits = own_ref[:, i : i + step] + dot(left, right, 1, 1)
        out_ref[:, i : i + step] = logits
        peak = jnp.max(logits, axis=0, keepdims=True)
        weights = jnp.exp(logits - peak)
        total = jnp.sum(weights, axis=0, keepdims=True)
        stats_ref[:, i : i + step] = peak + jnp.log(total)
        target = jnp.sum(logits * dense_ref[:, i : i + step], axis=0, keepdims=True)
        stats_ref[:, tokens + i : tokens + i + step] = target
        mean = jnp.sum(weights * logits, axis=0, keepdims=True) / total
        stats_ref[:, 2 * tokens + i : 2 * tokens + i + step] = mean


def logits_call(blocks, rows, weight, own, dense):
    count, tokens, half = rows[0].shape
    width = weight.shape[0]
    return call(
        functools.partial(logits_rest_kernel, step=256), "logits_rest",
        [array((width, tokens), f32), array((1, 3 * tokens), f32)], *rows, weight, own, dense,
        prefetch=(blocks,), flops=4 * count * tokens * half * width, size=8 * 2**20,
    )


def grad_kernel(
    block_ref, stats_ref, logits_ref, dense_ref, logprob_ref, weight_ref, grad_ref, turned_ref, out_ref, pad_ref
):
    width, tokens = logits_ref.shape
    step = pad_ref.shape[1]
    pad_ref[...] = jnp.zeros(pad_ref.shape, f32)
    for i in range(0, tokens, step):
        totals = stats_ref[:, i : i + step]
        peak = jnp.max(totals, axis=0, keepdims=True)
        total = peak + jnp.log(jnp.sum(jnp.exp(totals - peak), axis=0, keepdims=True))
        mass = jnp.sum(jnp.exp(logprob_ref[:, i : i + step]), axis=0, keepdims=True)
        student = mass * jnp.exp(logits_ref[:, i : i + step] - total)
        grad = loss_scale * (student - dense_ref[:, i : i + step])
        grad_ref[:, i : i + step] = grad.astype(bf16)
        pad_ref[:width, :] = grad
        turned_ref[i : i + step, :] = pad_ref[...].T[:, :width].astype(bf16)
    rest_kernel(block_ref, turned_ref, weight_ref, out_ref, second=0)


def feature_part(weight_ref, blocks_ref, k, second):
    half = weight_ref.shape[1] // (4 * NY)
    return weight_ref[:, pl.ds(pl.multiple_of(blocks_ref[k] * 2 * half + second * half, 256), half)]


def grad_call(blocks, stats, logits, dense, logprob, weight):
    width, tokens = logits.shape
    count = blocks.shape[0]
    half = weight.shape[1] // (4 * count)
    inside = pl.BlockSpec(memory_space=pltpu.VMEM)
    return call(
        grad_kernel, "grad_logits",
        [array((width, tokens), bf16), array((tokens, width), bf16), array((count, tokens, half), bf16)],
        stats, logits, dense, logprob, weight, prefetch=(blocks,), ins=[inside] * 5, outs=[inside] * 3,
        scratch=[pltpu.VMEM((-(-width // 128) * 128, 128), f32)],
        flops=2 * count * tokens * half * width, size=12 * 2**20,
    )


def rest_kernel(block_ref, turned_ref, weight_ref, out_ref, *, second):
    for k in range(out_ref.shape[0]):
        out_ref[k] = dot(turned_ref[...], feature_part(weight_ref, block_ref, k, second)).astype(bf16)


def add_kernel(block_ref, turned_ref, weight_ref, other_ref, out_ref, *, second):
    for k in range(out_ref.shape[0]):
        out = dot(turned_ref[...], feature_part(weight_ref, block_ref, k, second))
        out_ref[k] = (out + other_ref[k].astype(f32)).astype(bf16)


def own_kernel(block_ref, at_ref, turned_ref, weight_ref, first_ref, second_ref, out_ref, *refs):
    add_kernel(block_ref, turned_ref, weight_ref, first_ref, out_ref, second=0)
    by_x, keep_ref = refs[:4], refs[4]
    rows = keep_ref.shape[2]
    for y in range(second_ref.shape[0]):
        out = dot(turned_ref[...], feature_part(weight_ref, block_ref, y, 1))
        out = (out + second_ref[y].astype(f32)).astype(bf16)
        for k in range(4):
            keep_ref[k, y] = out[k * rows : (k + 1) * rows]
    for k in range(4):
        by_x[k][...] = keep_ref[(at_ref[0] + k) % 4]


def rest_call(blocks, turned, weight):
    tokens, width = turned.shape
    count = blocks.shape[0]
    half = weight.shape[1] // (4 * count)
    return call(
        functools.partial(rest_kernel, second=1), "grad_rest", array((count, tokens, half), bf16), turned, weight,
        prefetch=(blocks,), flops=2 * count * tokens * half * width, size=6 * 2**20,
    )


def own_call(blocks, at, turned, weight, first, second):
    tokens, width = turned.shape
    count, _, half = first.shape
    rows = tokens // NX
    inside = pl.BlockSpec(memory_space=pltpu.VMEM)
    return call(
        own_kernel, "grad_own", [array(first.shape, bf16)] + [array((count, rows, half), bf16)] * 4,
        turned, weight, first, second, prefetch=(blocks, at), ins=[inside] * 4, outs=[inside] * 5,
        scratch=[pltpu.VMEM((NX, count, rows, half), bf16)],
        flops=4 * count * tokens * half * width, size=12 * 2**20,
    )


def sum_kernel(at_ref, by_y_ref, *refs):
    by_x, to_x, to_y_ref, keep_ref = refs[:4], refs[4:8], refs[8], refs[9]
    count, rows = by_x[0].shape[:2]
    for i in range(count):
        part = pl.ds(i * rows, rows)
        keep_ref[i] = sum(by_y_ref[j, part, :].astype(f32) for j in range(count)).astype(bf16)
        to_y_ref[i] = sum(r[i].astype(f32) for r in by_x).astype(bf16)
    for k in range(4):
        to_x[k][...] = keep_ref[(at_ref[0] + k) % 4]


def tokens_kernel(stats_ref, logprob_ref, kl_ref, dots_ref):
    tokens = kl_ref.shape[1]
    logprob = logprob_ref[...]
    prob = jnp.exp(logprob)
    mass = jnp.sum(prob, axis=0, keepdims=True)
    totals = stats_ref[:, :tokens]
    peak = jnp.max(totals, axis=0, keepdims=True)
    weights = jnp.exp(totals - peak)
    total = jnp.sum(weights, axis=0, keepdims=True)
    target = jnp.sum(stats_ref[:, tokens : 2 * tokens], axis=0, keepdims=True)
    mean = jnp.sum(weights * stats_ref[:, 2 * tokens :], axis=0, keepdims=True) / total
    kl_ref[...] = jnp.sum(prob * logprob, axis=0, keepdims=True) - target + mass * (peak + jnp.log(total))
    dots_ref[...] = loss_scale * (mass * mean - target)


def spread_kernel(*refs):
    by_x, (by_y_ref, spread_ref, out_ref) = refs[:4], refs[4:]
    first = sum(r[...].astype(f32) for r in by_x)
    second = sum(by_y_ref[j].astype(f32) for j in range(by_y_ref.shape[0]))
    both = jnp.concatenate([first.astype(bf16), second.astype(bf16)], axis=1)
    turns = out_ref.shape[1]
    slots = NX * turns
    for z in range(out_ref.shape[0] // NX):
        rows = dot(spread_ref[z * slots : (z + 1) * slots, :].astype(bf16), both).astype(bf16)
        for k in range(NX):
            out_ref[z * NX + k] = rows[k * turns : (k + 1) * turns]


def finish_kernel(at_ref, got_ref, rows_ref, gain_ref, dots_ref, out_ref, sum_ref, grad_ref):
    offset, count = own_slots(at_ref)
    turns, share = sum_ref.shape[1:]
    slots, features = rows_ref.shape
    tokens = dots_ref.shape[1]
    for k in range(NX):
        total = got_ref[k].astype(f32)
        for z in range(1, got_ref.shape[0] // NX):
            total += got_ref[z * NX + k].astype(f32)
        sum_ref[k] = total
    for i in range(NX):
        for m in range(turns):
            grad_ref[NX * m + i : NX * m + i + 1, :] = sum_ref[(offset + i) & (NX - 1), m : m + 1, :]
    rank = offset + lax.broadcasted_iota(jnp.int32, (slots, tokens), 0)
    row = (rank & (NX - 1)) * (tokens // NX) + ((rank & (GROUPS - 1)) >> 2) * (tokens // GROUPS) + (rank >> 5)
    here = row == lax.broadcasted_iota(jnp.int32, (slots, tokens), 1)
    dots = jnp.sum(jnp.where(here, dots_ref[...], 0.0), axis=1, keepdims=True)
    part = pl.ds(pl.multiple_of(at_ref[3] * share, share), share)
    inv_rms = inverse_rms(rows_ref, share)
    grad = (grad_ref[...] * gain_ref[:, part] - rows_ref[:, part].astype(f32) * (inv_rms * dots / features)) * inv_rms
    live = lax.broadcasted_iota(jnp.int32, grad.shape, 0) < count
    out_ref[...] = jnp.where(live, grad, 0.0).astype(bf16)


def weight_grad_kernel(block_ref, *refs):
    own, rest, grad_ref, out_ref = refs[:2], refs[2:4], refs[4], refs[5]

    def write(rows):
        half = rows[0].shape[2]
        for h in range(2):
            out_ref[:, h * half : (h + 1) * half] = dot(grad_ref[...], rows[h][0]).astype(bf16)

    count = pl.num_programs(0) // 2

    @pl.when(pl.program_id(0) < count)
    def _():
        write(own)

    @pl.when(pl.program_id(0) >= count)
    def _():
        write(rest)


def weight_grad(blocks, own, rest, grad):
    count, tokens, half = own[0].shape
    width = grad.shape[0]
    return call(
        weight_grad_kernel, "weight_grad", array((width, 4 * count * half), bf16), *own, *rest, grad,
        grid=(2 * count,), prefetch=(blocks,),
        ins=[
            *[pl.BlockSpec((1, tokens, half), lambda k, b: (jnp.minimum(k, count - 1), 0, 0))] * 2,
            *[pl.BlockSpec((1, tokens, half), lambda k, b: (jnp.maximum(k - count, 0), 0, 0))] * 2,
            pl.BlockSpec((width, tokens), lambda k, b: (0, 0)),
        ],
        outs=pl.BlockSpec((width, 2 * half), lambda k, b: (0, b[k])),
        flops=8 * count * tokens * half * width, size=16 * 2**20,
    )


def after(small, *others):
    return lax.optimization_barrier((small, others))[0]


def exchange(x, axis, lines=None):
    return lax.all_to_all(x, axis, 0, 0, tiled=True, axis_index_groups=lines)


def along_x(x, k):
    return lax.ppermute(x, "seq", [(i, i // NX * NX + (i + k) % NX) for i in range(GROUPS)])


def along_y(x, k):
    return lax.ppermute(x, "vocab", [(i, (i + 2 * k) % (2 * NY)) for i in range(2 * NY)])


def from_ahead(x, move):
    got = {k: move(x, -k) for k in STEPS}
    return [x, got[1], got[2], got[3]]


def to_ahead(pieces, move):
    return [pieces[0], *(move(pieces[k], k) for k in STEPS)]


def merge(stats):
    tokens = stats[0].shape[1] // 3
    totals = [s[:, :tokens] for s in stats]
    peak = totals[0]
    for t in totals[1:]:
        peak = jnp.maximum(peak, t)
    weights = [jnp.exp(t - peak) for t in totals]
    total = sum(weights)
    target = sum(s[:, tokens : 2 * tokens] for s in stats)
    mean = sum(w * s[:, 2 * tokens :] for w, s in zip(weights, stats)) / total
    return jnp.concatenate([peak + jnp.log(total), target, mean], axis=1)


def per_device(rollout, group_count, final_gain, head_weight, teacher_index, teacher_logprob):
    slots, features = rollout.shape
    tokens, entries = teacher_index.shape
    width = head_weight.shape[1]
    weight = head_weight.T
    parts = 2 * NY
    share = features // parts
    half = share // 2
    class_rows = tokens // NX
    turns = slots // NX
    pack_rows = tokens // GROUPS
    seq = lax.axis_index("seq")
    own_z, own_x = seq // NX, seq % NX
    vocab = lax.axis_index("vocab")
    own_y, core = vocab // 2, vocab % 2
    at = jnp.concatenate([jnp.stack([own_x, own_y, seq, vocab]).astype(jnp.int32), group_count])

    of_class = call(
        sort_kernel, "sort_rows", array((GROUPS, turns, share), bf16), rollout, final_gain[None, :], prefetch=(at,), size=2**19
    )
    of_class = exchange(of_class, "seq")

    def class_order(a):
        return a.reshape(NZ, NX, pack_rows, entries).transpose(1, 0, 2, 3).reshape(tokens, entries).T

    index = class_order(teacher_index)
    logprob = class_order(teacher_logprob)
    first_column = (seq * parts + vocab) * width
    dense = teacher_columns(first_column, index, logprob, width)

    group_ids = jnp.arange(GROUPS, dtype=jnp.int32)
    before = group_ids[None, :] < group_ids[:, None]
    offsets = jnp.sum(jnp.where(before, group_count[None, :], 0), axis=1)
    turn_ids = jnp.arange(turns, dtype=jnp.int32)
    row_in_group = (own_x - offsets[:, None]) % NX + NX * turn_ids[None, :]
    rank = offsets[:, None] + row_in_group
    place = jnp.where(row_in_group < group_count[:, None], rank % GROUPS // NX * pack_rows + rank // GROUPS, class_rows)
    place_ids = jnp.arange(class_rows, dtype=jnp.int32)
    place = after(place, dense)
    spread = lax.optimization_barrier((place.reshape(-1, 1) == place_ids[None, :]).astype(f32))
    dense_rows = dot(spread.astype(bf16), of_class.reshape(-1, share), 0, 0).astype(bf16)

    by_x = from_ahead(dense_rows[:, :half], along_x)
    all_y = exchange(jnp.broadcast_to(dense_rows[:, half:], (NY, class_rows, half)), "vocab", Y_LINES)
    all_x = call(place_kernel, "place", array((NY, NX, class_rows, half), bf16), *by_x, prefetch=(at,), size=2**21)
    by_x = from_ahead(all_y, along_x)
    own_first = exchange(all_x.reshape(NY, tokens, half), "vocab", Y_LINES)

    y_ids = jnp.arange(NY, dtype=jnp.int32)
    own_blocks = 2 * y_ids + core
    rest_blocks = 2 * y_ids + 1 - core
    own_second = call(
        gather_kernel, "gather_rows", array((NY, NX, class_rows, half), bf16), *by_x, prefetch=(at,), size=2**22
    ).reshape(NY, tokens, half)
    rest_second = lax.ppermute(own_second, "vocab", OTHER_CORE)
    logits_own = half_logits(own_blocks, 1, own_second, weight)
    rest_first = lax.ppermute(own_first, "vocab", OTHER_CORE)
    logits_own = half_logits(after(own_blocks, logits_own), 0, own_first, weight, logits_own)
    own_rows, rest_rows = [own_first, own_second], [rest_first, rest_second]
    logits, stats = logits_call(rest_blocks, rest_rows, weight, logits_own, dense)
    stats = merge([stats, lax.ppermute(stats, "vocab", OTHER_CORE)])
    stats = merge(from_ahead(stats, along_y))
    stats = exchange(jnp.broadcast_to(stats, (GROUPS, 3 * tokens)), "seq")

    grad, turned, rest_first = grad_call(rest_blocks, stats, logits, dense, logprob, weight)
    other_first = lax.ppermute(rest_first, "vocab", OTHER_CORE)
    other_second = lax.ppermute(rest_call(rest_blocks, turned, weight), "vocab", OTHER_CORE)
    first, *pieces = own_call(own_blocks, at, turned, weight, other_first, other_second)
    by_y = exchange(first, "vocab", Y_LINES)
    by_x = to_ahead(pieces, along_x)
    weight_t = weight_grad(after(jnp.concatenate([own_blocks, rest_blocks]), pieces), own_rows, rest_rows, grad)
    kl, dots = call(tokens_kernel, "tokens", [array((1, tokens), f32)] * 2, stats, logprob, size=2**19)
    kl = lax.dynamic_slice_in_dim(kl[0], own_x * class_rows + own_z * pack_rows, pack_rows)
    at = after(at, weight_t, kl, dots)

    small = array((class_rows, half), bf16)
    inside = pl.BlockSpec(memory_space=pltpu.VMEM)
    *pieces, to_y = call(
        sum_kernel, "add_pieces", [small] * 4 + [array((NY, class_rows, half), bf16)], by_y, *by_x, prefetch=(at,),
        ins=[inside] * 5, outs=[inside] * 5, scratch=[pltpu.VMEM((NX, class_rows, half), bf16)], size=2**22,
    )
    by_x = to_ahead(pieces, along_x)
    by_y = exchange(to_y, "vocab", Y_LINES)
    spread_grad = call(
        spread_kernel, "spread_rows", array((GROUPS, turns, share), bf16), *by_x, by_y, spread, size=2**20
    )
    grad_rollout = call(
        finish_kernel, "finish", array((slots, share), bf16), exchange(spread_grad, "seq"), rollout, final_gain[None, :],
        dots, prefetch=(at,), ins=[inside] * 4, outs=inside,
        scratch=[pltpu.VMEM((NX, turns, share), f32), pltpu.VMEM((slots, share), f32)], size=2**19,
    )
    return (kl, weight_t.T, grad_rollout)


def solution(mesh):
    placed = (P("seq", None), P(), P(), P(None, ("seq", "vocab")), P(), P())
    return jax.shard_map(
        per_device,
        mesh=mesh,
        in_specs=placed,
        out_specs=(P("seq"), P(None, ("seq", "vocab")), P("seq", "vocab")),
        check_vma=False,
    )
```

```python
import functools

import jax
import jax.numpy as jnp
from jax import lax
from jax.experimental import pallas as pl
from jax.experimental.pallas import tpu as pltpu
from jax.sharding import PartitionSpec as P

norm_eps = 1e-06
loss_scale = 16.0
f32, bf16 = jnp.float32, jnp.bfloat16

NX, NY, NZ = 4, 4, 8
GROUPS = NX * NZ
Y_LINES = [[y * 2 + core for y in range(NY)] for core in range(2)]
OTHER_CORE = [(i, i ^ 1) for i in range(2 * NY)]
STEPS = (1, 3, 2)
VMEM = 24 * 2**20


def call(body, name, out, *operands, grid=(), prefetch=(), ins=None, outs=None, scratch=(), flops=0, size=0):
    whole = pl.BlockSpec(memory_space=pltpu.VMEM)
    if ins is None:
        ins, outs = [whole] * len(operands), jax.tree.map(lambda _: whole, out)
    return pl.pallas_call(
        body,
        grid_spec=pltpu.PrefetchScalarGridSpec(
            num_scalar_prefetch=len(prefetch), grid=grid, in_specs=ins, out_specs=outs, scratch_shapes=scratch
        ),
        out_shape=out,
        cost_estimate=pl.CostEstimate(flops=flops, bytes_accessed=size, transcendentals=0),
        compiler_params=pltpu.CompilerParams(vmem_limit_bytes=VMEM),
        name=name,
    )(*prefetch, *operands)


def array(shape, dtype):
    return jax.ShapeDtypeStruct(shape, dtype)


def dot(a, b, over_a=1, over_b=0):
    return lax.dot_general(a, b, (((over_a,), (over_b,)), ((), ())), preferred_element_type=f32)


def own_slots(at_ref):
    seq = at_ref[2]
    offset = lax.fori_loop(0, GROUPS, lambda g, o: o + jnp.where(g < seq, at_ref[4 + g], 0), jnp.int32(0))
    return offset, at_ref[4 + seq]


def inverse_rms(rows_ref, step):
    slots, features = rows_ref.shape
    square = jnp.zeros((slots, step), f32)
    for i in range(0, features, step):
        values = rows_ref[:, i : i + step].astype(f32)
        square += values * values
    return lax.rsqrt(jnp.sum(square, axis=1, keepdims=True) / features + norm_eps)


def sort_kernel(at_ref, rows_ref, gain_ref, out_ref):
    vocab = at_ref[3]
    slots, features = rows_ref.shape
    turns, share = out_ref.shape[1:]
    offset, count = own_slots(at_ref)
    inv_rms = inverse_rms(rows_ref, share)
    part = pl.ds(pl.multiple_of(vocab * share, share), share)
    normed = (rows_ref[:, part].astype(f32) * inv_rms * gain_ref[:, part]).astype(bf16)
    to = lax.broadcasted_iota(jnp.int32, (slots, slots), 0)
    source = lax.broadcasted_iota(jnp.int32, (slots, slots), 1)
    kind = sum((to >= i * turns).astype(jnp.int32) for i in range(1, NX))
    row = ((kind - offset) & (NX - 1)) + NX * (to - kind * turns)
    pick = jnp.where((row == source) & (row < count), 1.0, 0.0).astype(bf16)
    by_class = dot(pick, normed).astype(bf16)
    for g in range(out_ref.shape[0]):
        k = g % NX
        out_ref[g] = by_class[k * turns : (k + 1) * turns]


def teacher_kernel(first_ref, index_ref, logprob_ref, dense_ref):
    local = index_ref[...] - first_ref[0]
    prob = jnp.exp(logprob_ref[...])
    width, tokens = dense_ref.shape
    step = 200
    for start in range(0, width, step):
        size = min(step, width - start)
        ids = lax.broadcasted_iota(jnp.int32, (size, tokens), 0) + start
        dense = jnp.zeros((size, tokens), f32)
        for j in range(local.shape[0]):
            dense = jnp.where(local[j : j + 1, :] == ids, prob[j : j + 1, :], dense)
        dense_ref[start : start + size, :] = dense


def teacher_columns(first_column, index, logprob, width):
    entries, tokens = index.shape
    block = 128
    return call(
        teacher_kernel, "teacher_columns", array((width, tokens), f32), index, logprob,
        grid=(tokens // block,), prefetch=(first_column.reshape(1),),
        ins=[pl.BlockSpec((entries, block), lambda i, s: (0, i))] * 2,
        outs=pl.BlockSpec((width, block), lambda i, s: (0, i)),
        flops=4 * tokens * width * entries, size=4 * tokens * width,
    )


def place_kernel(at_ref, *refs):
    by_x, out_ref = refs[:4], refs[4]
    for k in range(4):
        piece = by_x[k][...]
        for y in range(4):
            out_ref[y, (at_ref[0] + k) % 4] = piece


def gather_kernel(at_ref, *refs):
    by_x, out_ref = refs[:4], refs[4]
    for k in range(4):
        for y in range(4):
            out_ref[y, (at_ref[0] + k) % 4] = by_x[k][y]


def columns(weight_ref, blocks_ref, start, size):
    width = weight_ref.shape[1] // (2 * NY)
    parts = [pl.ds(pl.multiple_of(blocks_ref[k] * width + start, 256), size) for k in range(NY)]
    return jnp.concatenate([weight_ref[:, p] for p in parts], axis=1)


def side_by_side(rows_ref, part):
    return jnp.concatenate([rows_ref[k, part, :] for k in range(rows_ref.shape[0])], axis=1)


def half_logits_kernel(block_ref, rows_ref, weight_ref, *refs, second, step):
    out_ref = refs[-1]
    half = rows_ref.shape[2]
    left = columns(weight_ref, block_ref, second * half, half)
    for i in range(0, out_ref.shape[1], step):
        part = dot(left, side_by_side(rows_ref, pl.ds(i, step)), 1, 1)
        out_ref[:, i : i + step] = part if len(refs) == 1 else refs[0][:, i : i + step] + part


def half_logits(blocks, second, rows, weight, *before):
    count, tokens, half = rows.shape
    width = weight.shape[0]
    body = functools.partial(half_logits_kernel, second=second, step=256)
    return call(
        body, "logits_half", array((width, tokens), f32), rows, weight, *before,
        prefetch=(blocks,), flops=2 * count * tokens * half * width, size=6 * 2**20,
    )


def logits_rest_kernel(block_ref, first_ref, second_ref, weight_ref, own_ref, dense_ref, out_ref, stats_ref, *, step):
    tokens, half = out_ref.shape[1], first_ref.shape[2]
    left = jnp.concatenate([columns(weight_ref, block_ref, h * half, half) for h in range(2)], axis=1)
    for i in range(0, tokens, step):
        here = pl.ds(i, step)
        right = jnp.concatenate([side_by_side(first_ref, here), side_by_side(second_ref, here)], axis=1)
        logits = own_ref[:, i : i + step] + dot(left, right, 1, 1)
        out_ref[:, i : i + step] = logits
        peak = jnp.max(logits, axis=0, keepdims=True)
        weights = jnp.exp(logits - peak)
        total = jnp.sum(weights, axis=0, keepdims=True)
        stats_ref[:, i : i + step] = peak + jnp.log(total)
        target = jnp.sum(logits * dense_ref[:, i : i + step], axis=0, keepdims=True)
        stats_ref[:, tokens + i : tokens + i + step] = target
        mean = jnp.sum(weights * logits, axis=0, keepdims=True) / total
        stats_ref[:, 2 * tokens + i : 2 * tokens + i + step] = mean


def logits_call(blocks, rows, weight, own, dense):
    count, tokens, half = rows[0].shape
    width = weight.shape[0]
    return call(
        functools.partial(logits_rest_kernel, step=256), "logits_rest",
        [array((width, tokens), f32), array((1, 3 * tokens), f32)], *rows, weight, own, dense,
        prefetch=(blocks,), flops=4 * count * tokens * half * width, size=8 * 2**20,
    )


def grad_kernel(
    block_ref, stats_ref, logits_ref, dense_ref, logprob_ref, weight_ref, grad_ref, turned_ref, out_ref, pad_ref
):
    width, tokens = logits_ref.shape
    step = pad_ref.shape[1]
    pad_ref[...] = jnp.zeros(pad_ref.shape, f32)
    for i in range(0, tokens, step):
        totals = stats_ref[:, i : i + step]
        peak = jnp.max(totals, axis=0, keepdims=True)
        total = peak + jnp.log(jnp.sum(jnp.exp(totals - peak), axis=0, keepdims=True))
        mass = jnp.sum(jnp.exp(logprob_ref[:, i : i + step]), axis=0, keepdims=True)
        student = mass * jnp.exp(logits_ref[:, i : i + step] - total)
        grad = loss_scale * (student - dense_ref[:, i : i + step])
        grad_ref[:, i : i + step] = grad.astype(bf16)
        pad_ref[:width, :] = grad
        turned_ref[i : i + step, :] = pad_ref[...].T[:, :width].astype(bf16)
    rest_kernel(block_ref, turned_ref, weight_ref, out_ref, second=0)


def feature_part(weight_ref, blocks_ref, k, second):
    half = weight_ref.shape[1] // (4 * NY)
    return weight_ref[:, pl.ds(pl.multiple_of(blocks_ref[k] * 2 * half + second * half, 256), half)]


def grad_call(blocks, stats, logits, dense, logprob, weight):
    width, tokens = logits.shape
    count = blocks.shape[0]
    half = weight.shape[1] // (4 * count)
    inside = pl.BlockSpec(memory_space=pltpu.VMEM)
    return call(
        grad_kernel, "grad_logits",
        [array((width, tokens), bf16), array((tokens, width), bf16), array((count, tokens, half), bf16)],
        stats, logits, dense, logprob, weight, prefetch=(blocks,), ins=[inside] * 5, outs=[inside] * 3,
        scratch=[pltpu.VMEM((-(-width // 128) * 128, 128), f32)],
        flops=2 * count * tokens * half * width, size=12 * 2**20,
    )


def rest_kernel(block_ref, turned_ref, weight_ref, out_ref, *, second):
    for k in range(out_ref.shape[0]):
        out_ref[k] = dot(turned_ref[...], feature_part(weight_ref, block_ref, k, second)).astype(bf16)


def add_kernel(block_ref, turned_ref, weight_ref, other_ref, out_ref, *, second):
    for k in range(out_ref.shape[0]):
        out = dot(turned_ref[...], feature_part(weight_ref, block_ref, k, second))
        out_ref[k] = (out + other_ref[k].astype(f32)).astype(bf16)


def split_kernel(block_ref, at_ref, turned_ref, weight_ref, other_ref, *refs, second):
    by_x, keep_ref = refs[:4], refs[4]
    rows = keep_ref.shape[2]
    for y in range(other_ref.shape[0]):
        out = dot(turned_ref[...], feature_part(weight_ref, block_ref, y, second))
        out = (out + other_ref[y].astype(f32)).astype(bf16)
        for k in range(4):
            keep_ref[k, y] = out[k * rows : (k + 1) * rows]
    for k in range(4):
        by_x[k][...] = keep_ref[(at_ref[0] + k) % 4]


def half_call(body, name, blocks, second, turned, weight, *other, at=None):
    tokens, width = turned.shape
    count = blocks.shape[0]
    half = weight.shape[1] // (4 * count)
    rows = tokens // NX
    inside = pl.BlockSpec(memory_space=pltpu.VMEM)
    if at is None:
        out, outs, scratch, prefetch = array((count, tokens, half), bf16), inside, (), (blocks,)
    else:
        out, outs = [array((count, rows, half), bf16)] * 4, [inside] * 4
        scratch, prefetch = [pltpu.VMEM((NX, count, rows, half), bf16)], (blocks, at)
    return call(
        functools.partial(body, second=second), name, out, turned, weight, *other, prefetch=prefetch, scratch=scratch,
        ins=[inside] * (2 + len(other)), outs=outs, flops=2 * count * tokens * half * width, size=6 * 2**20,
    )


def sum_kernel(at_ref, by_y_ref, *refs):
    by_x, to_x, to_y_ref, keep_ref = refs[:4], refs[4:8], refs[8], refs[9]
    count, rows = by_x[0].shape[:2]
    for i in range(count):
        part = pl.ds(i * rows, rows)
        keep_ref[i] = sum(by_y_ref[j, part, :].astype(f32) for j in range(count)).astype(bf16)
        to_y_ref[i] = sum(r[i].astype(f32) for r in by_x).astype(bf16)
    for k in range(4):
        to_x[k][...] = keep_ref[(at_ref[0] + k) % 4]


def tokens_kernel(stats_ref, logprob_ref, kl_ref, dots_ref):
    tokens = kl_ref.shape[1]
    logprob = logprob_ref[...]
    prob = jnp.exp(logprob)
    mass = jnp.sum(prob, axis=0, keepdims=True)
    totals = stats_ref[:, :tokens]
    peak = jnp.max(totals, axis=0, keepdims=True)
    weights = jnp.exp(totals - peak)
    total = jnp.sum(weights, axis=0, keepdims=True)
    target = jnp.sum(stats_ref[:, tokens : 2 * tokens], axis=0, keepdims=True)
    mean = jnp.sum(weights * stats_ref[:, 2 * tokens :], axis=0, keepdims=True) / total
    kl_ref[...] = jnp.sum(prob * logprob, axis=0, keepdims=True) - target + mass * (peak + jnp.log(total))
    dots_ref[...] = loss_scale * (mass * mean - target)


def spread_kernel(*refs):
    by_x, (by_y_ref, spread_ref, out_ref) = refs[:4], refs[4:]
    first = sum(r[...].astype(f32) for r in by_x)
    second = sum(by_y_ref[j].astype(f32) for j in range(by_y_ref.shape[0]))
    both = jnp.concatenate([first.astype(bf16), second.astype(bf16)], axis=1)
    slots, lanes = out_ref.shape[1:]
    turns = slots // NX
    for z in range(out_ref.shape[0] // NX):
        rows = dot(spread_ref[z * slots : (z + 1) * slots, :].astype(bf16), both).astype(bf16)
        for k in range(NX):
            for i in range(both.shape[1] // lanes):
                out_ref[z * NX + k, i * turns : (i + 1) * turns, :] = rows[
                    k * turns : (k + 1) * turns, i * lanes : (i + 1) * lanes
                ]


def finish_kernel(at_ref, got_ref, rows_ref, gain_ref, dots_ref, out_ref, sum_ref, grad_ref):
    offset, count = own_slots(at_ref)
    lanes, share = sum_ref.shape[2], grad_ref.shape[1]
    slots, features = rows_ref.shape
    turns = slots // NX
    tokens = dots_ref.shape[1]
    for k in range(NX):
        total = got_ref[k].astype(f32)
        for z in range(1, got_ref.shape[0] // NX):
            total += got_ref[z * NX + k].astype(f32)
        sum_ref[k] = total
    for i in range(NX):
        for m in range(turns):
            for j in range(share // lanes):
                row = j * turns + m
                grad_ref[NX * m + i : NX * m + i + 1, j * lanes : (j + 1) * lanes] = sum_ref[
                    (offset + i) & (NX - 1), row : row + 1, :
                ]
    rank = offset + lax.broadcasted_iota(jnp.int32, (slots, tokens), 0)
    row = (rank & (NX - 1)) * (tokens // NX) + ((rank & (GROUPS - 1)) >> 2) * (tokens // GROUPS) + (rank >> 5)
    here = row == lax.broadcasted_iota(jnp.int32, (slots, tokens), 1)
    dots = jnp.sum(jnp.where(here, dots_ref[...], 0.0), axis=1, keepdims=True)
    part = pl.ds(pl.multiple_of(at_ref[3] * share, share), share)
    inv_rms = inverse_rms(rows_ref, share)
    grad = (grad_ref[...] * gain_ref[:, part] - rows_ref[:, part].astype(f32) * (inv_rms * dots / features)) * inv_rms
    live = lax.broadcasted_iota(jnp.int32, grad.shape, 0) < count
    out_ref[...] = jnp.where(live, grad, 0.0).astype(bf16)


def weight_grad_kernel(block_ref, *refs):
    own, rest, grad_ref, out_ref = refs[:2], refs[2:4], refs[4], refs[5]

    def write(rows):
        half = rows[0].shape[2]
        for h in range(2):
            out_ref[:, h * half : (h + 1) * half] = dot(grad_ref[...], rows[h][0]).astype(bf16)

    count = pl.num_programs(0) // 2

    @pl.when(pl.program_id(0) < count)
    def _():
        write(own)

    @pl.when(pl.program_id(0) >= count)
    def _():
        write(rest)


def weight_grad(blocks, own, rest, grad):
    count, tokens, half = own[0].shape
    width = grad.shape[0]
    return call(
        weight_grad_kernel, "weight_grad", array((width, 4 * count * half), bf16), *own, *rest, grad,
        grid=(2 * count,), prefetch=(blocks,),
        ins=[
            *[pl.BlockSpec((1, tokens, half), lambda k, b: (jnp.minimum(k, count - 1), 0, 0))] * 2,
            *[pl.BlockSpec((1, tokens, half), lambda k, b: (jnp.maximum(k - count, 0), 0, 0))] * 2,
            pl.BlockSpec((width, tokens), lambda k, b: (0, 0)),
        ],
        outs=pl.BlockSpec((width, 2 * half), lambda k, b: (0, b[k])),
        flops=8 * count * tokens * half * width, size=16 * 2**20,
    )


def after(small, *others):
    return lax.optimization_barrier((small, others))[0]


def exchange(x, axis, lines=None):
    return lax.all_to_all(x, axis, 0, 0, tiled=True, axis_index_groups=lines)


def along_x(x, k):
    return lax.ppermute(x, "seq", [(i, i // NX * NX + (i + k) % NX) for i in range(GROUPS)])


def along_y(x, k):
    return lax.ppermute(x, "vocab", [(i, (i + 2 * k) % (2 * NY)) for i in range(2 * NY)])


def from_ahead(x, move):
    got = {k: move(x, -k) for k in STEPS}
    return [x, got[1], got[2], got[3]]


def to_ahead(pieces, move):
    return [pieces[0], *(move(pieces[k], k) for k in STEPS)]


def merge(stats):
    tokens = stats[0].shape[1] // 3
    totals = [s[:, :tokens] for s in stats]
    peak = totals[0]
    for t in totals[1:]:
        peak = jnp.maximum(peak, t)
    weights = [jnp.exp(t - peak) for t in totals]
    total = sum(weights)
    target = sum(s[:, tokens : 2 * tokens] for s in stats)
    mean = sum(w * s[:, 2 * tokens :] for w, s in zip(weights, stats)) / total
    return jnp.concatenate([peak + jnp.log(total), target, mean], axis=1)


def per_device(rollout, group_count, final_gain, head_weight, teacher_index, teacher_logprob):
    slots, features = rollout.shape
    tokens, entries = teacher_index.shape
    width = head_weight.shape[1]
    weight = head_weight.T
    parts = 2 * NY
    share = features // parts
    half = share // 2
    class_rows = tokens // NX
    turns = slots // NX
    pack_rows = tokens // GROUPS
    seq = lax.axis_index("seq")
    own_z, own_x = seq // NX, seq % NX
    vocab = lax.axis_index("vocab")
    own_y, core = vocab // 2, vocab % 2
    at = jnp.concatenate([jnp.stack([own_x, own_y, seq, vocab]).astype(jnp.int32), group_count])

    of_class = call(
        sort_kernel, "sort_rows", array((GROUPS, turns, share), bf16), rollout, final_gain[None, :], prefetch=(at,), size=2**19
    )
    of_class = exchange(of_class, "seq")

    def class_order(a):
        return a.reshape(NZ, NX, pack_rows, entries).transpose(1, 0, 2, 3).reshape(tokens, entries).T

    index = class_order(teacher_index)
    logprob = class_order(teacher_logprob)
    first_column = (seq * parts + vocab) * width
    dense = teacher_columns(first_column, index, logprob, width)

    group_ids = jnp.arange(GROUPS, dtype=jnp.int32)
    before = group_ids[None, :] < group_ids[:, None]
    offsets = jnp.sum(jnp.where(before, group_count[None, :], 0), axis=1)
    turn_ids = jnp.arange(turns, dtype=jnp.int32)
    row_in_group = (own_x - offsets[:, None]) % NX + NX * turn_ids[None, :]
    rank = offsets[:, None] + row_in_group
    place = jnp.where(row_in_group < group_count[:, None], rank % GROUPS // NX * pack_rows + rank // GROUPS, class_rows)
    place_ids = jnp.arange(class_rows, dtype=jnp.int32)
    place = after(place, dense)
    spread = lax.optimization_barrier((place.reshape(-1, 1) == place_ids[None, :]).astype(f32))
    dense_rows = dot(spread.astype(bf16), of_class.reshape(-1, share), 0, 0).astype(bf16)

    by_x = from_ahead(dense_rows[:, :half], along_x)
    all_y = exchange(jnp.broadcast_to(dense_rows[:, half:], (NY, class_rows, half)), "vocab", Y_LINES)
    all_x = call(place_kernel, "place", array((NY, NX, class_rows, half), bf16), *by_x, prefetch=(at,), size=2**21)
    by_x = from_ahead(all_y, along_x)
    own_first = exchange(all_x.reshape(NY, tokens, half), "vocab", Y_LINES)

    y_ids = jnp.arange(NY, dtype=jnp.int32)
    own_blocks = 2 * y_ids + core
    rest_blocks = 2 * y_ids + 1 - core
    own_second = call(
        gather_kernel, "gather_rows", array((NY, NX, class_rows, half), bf16), *by_x, prefetch=(at,), size=2**22
    ).reshape(NY, tokens, half)
    rest_second = lax.ppermute(own_second, "vocab", OTHER_CORE)
    logits_own = half_logits(own_blocks, 1, own_second, weight)
    rest_first = lax.ppermute(own_first, "vocab", OTHER_CORE)
    logits_own = half_logits(after(own_blocks, logits_own), 0, own_first, weight, logits_own)
    own_rows, rest_rows = [own_first, own_second], [rest_first, rest_second]
    logits, stats = logits_call(rest_blocks, rest_rows, weight, logits_own, dense)
    stats = merge([stats, lax.ppermute(stats, "vocab", OTHER_CORE)])
    stats = merge(from_ahead(stats, along_y))
    stats = exchange(jnp.broadcast_to(stats, (GROUPS, 3 * tokens)), "seq")

    grad, turned, rest_first = grad_call(rest_blocks, stats, logits, dense, logprob, weight)
    other_first = lax.ppermute(rest_first, "vocab", OTHER_CORE)
    other_second = lax.ppermute(half_call(rest_kernel, "grad_rest", rest_blocks, 1, turned, weight), "vocab", OTHER_CORE)
    first = half_call(add_kernel, "grad_first", own_blocks, 0, turned, weight, other_first)
    by_y = exchange(first, "vocab", Y_LINES)
    pieces = half_call(split_kernel, "grad_second", after(own_blocks, first), 1, turned, weight, other_second, at=at)
    by_x = to_ahead(pieces, along_x)
    weight_t = weight_grad(after(jnp.concatenate([own_blocks, rest_blocks]), pieces), own_rows, rest_rows, grad)
    kl, dots = call(tokens_kernel, "tokens", [array((1, tokens), f32)] * 2, stats, logprob, size=2**19)
    kl = lax.dynamic_slice_in_dim(kl[0], own_x * class_rows + own_z * pack_rows, pack_rows)
    at = after(at, weight_t, kl, dots)

    small = array((class_rows, half), bf16)
    inside = pl.BlockSpec(memory_space=pltpu.VMEM)
    *pieces, to_y = call(
        sum_kernel, "add_pieces", [small] * 4 + [array((NY, class_rows, half), bf16)], by_y, *by_x, prefetch=(at,),
        ins=[inside] * 5, outs=[inside] * 5, scratch=[pltpu.VMEM((NX, class_rows, half), bf16)], size=2**22,
    )
    by_x = to_ahead(pieces, along_x)
    by_y = exchange(to_y, "vocab", Y_LINES)
    spread_grad = call(
        spread_kernel, "spread_rows", array((GROUPS, slots, share // NX), bf16), *by_x, by_y, spread, size=2**20
    )
    grad_rollout = call(
        finish_kernel, "finish", array((slots, share), bf16), exchange(spread_grad, "seq"), rollout, final_gain[None, :],
        dots, prefetch=(at,), ins=[inside] * 4, outs=inside,
        scratch=[pltpu.VMEM((NX, slots, share // NX), f32), pltpu.VMEM((slots, share), f32)], size=2**19,
    )
    return (kl, weight_t.T, grad_rollout)


def solution(mesh):
    placed = (P("seq", None), P(), P(), P(None, ("seq", "vocab")), P(), P())
    return jax.shard_map(
        per_device,
        mesh=mesh,
        in_specs=placed,
        out_specs=(P("seq"), P(None, ("seq", "vocab")), P("seq", "vocab")),
        check_vma=False,
    )
```

```python
import functools

import jax
import jax.numpy as jnp
from jax import lax
from jax.experimental import pallas as pl
from jax.experimental.pallas import tpu as pltpu
from jax.sharding import PartitionSpec as P

norm_eps = 1e-06
loss_scale = 16.0
f32, bf16 = jnp.float32, jnp.bfloat16

NX, NY, NZ = 4, 4, 8
GROUPS = NX * NZ
Y_LINES = [[y * 2 + core for y in range(NY)] for core in range(2)]
OTHER_CORE = [(i, i ^ 1) for i in range(2 * NY)]
STEPS = (1, 3, 2)
VMEM = 24 * 2**20


def call(body, name, out, *operands, grid=(), prefetch=(), ins=None, outs=None, scratch=(), flops=0, size=0):
    whole = pl.BlockSpec(memory_space=pltpu.VMEM)
    if ins is None:
        ins, outs = [whole] * len(operands), jax.tree.map(lambda _: whole, out)
    return pl.pallas_call(
        body,
        grid_spec=pltpu.PrefetchScalarGridSpec(
            num_scalar_prefetch=len(prefetch), grid=grid, in_specs=ins, out_specs=outs, scratch_shapes=scratch
        ),
        out_shape=out,
        cost_estimate=pl.CostEstimate(flops=flops, bytes_accessed=size, transcendentals=0),
        compiler_params=pltpu.CompilerParams(vmem_limit_bytes=VMEM),
        name=name,
    )(*prefetch, *operands)


def array(shape, dtype):
    return jax.ShapeDtypeStruct(shape, dtype)


def dot(a, b, over_a=1, over_b=0):
    return lax.dot_general(a, b, (((over_a,), (over_b,)), ((), ())), preferred_element_type=f32)


def own_slots(at_ref):
    seq = at_ref[2]
    offset = lax.fori_loop(0, GROUPS, lambda g, o: o + jnp.where(g < seq, at_ref[4 + g], 0), jnp.int32(0))
    return offset, at_ref[4 + seq]


def inverse_rms(rows_ref, step):
    slots, features = rows_ref.shape
    square = jnp.zeros((slots, step), f32)
    for i in range(0, features, step):
        values = rows_ref[:, i : i + step].astype(f32)
        square += values * values
    return lax.rsqrt(jnp.sum(square, axis=1, keepdims=True) / features + norm_eps)


def sort_kernel(at_ref, rows_ref, gain_ref, out_ref):
    vocab = at_ref[3]
    slots, features = rows_ref.shape
    turns, lanes, share = slots // NX, out_ref.shape[2], NX * out_ref.shape[2]
    offset, count = own_slots(at_ref)
    inv_rms = inverse_rms(rows_ref, share)
    part = pl.ds(pl.multiple_of(vocab * share, share), share)
    normed = (rows_ref[:, part].astype(f32) * inv_rms * gain_ref[:, part]).astype(bf16)
    to = lax.broadcasted_iota(jnp.int32, (slots, slots), 0)
    source = lax.broadcasted_iota(jnp.int32, (slots, slots), 1)
    kind = sum((to >= i * turns).astype(jnp.int32) for i in range(1, NX))
    row = ((kind - offset) & (NX - 1)) + NX * (to - kind * turns)
    pick = jnp.where((row == source) & (row < count), 1.0, 0.0).astype(bf16)
    by_class = dot(pick, normed).astype(bf16)
    for g in range(out_ref.shape[0]):
        k = g % NX
        for i in range(NX):
            out_ref[g, i * turns : (i + 1) * turns, :] = by_class[
                k * turns : (k + 1) * turns, i * lanes : (i + 1) * lanes
            ]


def compact_kernel(got_ref, spread_ref, first_ref, second_ref, rows_ref):
    count, slots, lanes = got_ref.shape
    turns = slots // NX
    for g in range(count):
        for i in range(NX):
            piece = got_ref[g, i * turns : (i + 1) * turns, :].astype(f32)
            rows_ref[g * turns : (g + 1) * turns, i * lanes : (i + 1) * lanes] = piece
    rows = dot(spread_ref[...].astype(bf16), rows_ref[...].astype(bf16), 0, 0).astype(bf16)
    half = first_ref.shape[1]
    first_ref[...] = rows[:, :half]
    for y in range(second_ref.shape[0]):
        second_ref[y] = rows[:, half:]


def teacher_kernel(first_ref, index_ref, logprob_ref, dense_ref):
    local = index_ref[...] - first_ref[0]
    prob = jnp.exp(logprob_ref[...])
    width, tokens = dense_ref.shape
    step = 200
    for start in range(0, width, step):
        size = min(step, width - start)
        ids = lax.broadcasted_iota(jnp.int32, (size, tokens), 0) + start
        dense = jnp.zeros((size, tokens), f32)
        for j in range(local.shape[0]):
            dense = jnp.where(local[j : j + 1, :] == ids, prob[j : j + 1, :], dense)
        dense_ref[start : start + size, :] = dense


def teacher_columns(first_column, index, logprob, width):
    entries, tokens = index.shape
    block = 128
    return call(
        teacher_kernel, "teacher_columns", array((width, tokens), f32), index, logprob,
        grid=(tokens // block,), prefetch=(first_column.reshape(1),),
        ins=[pl.BlockSpec((entries, block), lambda i, s: (0, i))] * 2,
        outs=pl.BlockSpec((width, block), lambda i, s: (0, i)),
        flops=4 * tokens * width * entries, size=4 * tokens * width,
    )


def place_kernel(at_ref, *refs):
    by_x, out_ref = refs[:4], refs[4]
    for k in range(4):
        piece = by_x[k][...]
        for y in range(4):
            out_ref[y, (at_ref[0] + k) % 4] = piece


def gather_kernel(at_ref, *refs):
    by_x, out_ref = refs[:4], refs[4]
    for k in range(4):
        for y in range(4):
            out_ref[y, (at_ref[0] + k) % 4] = by_x[k][y]


def columns(weight_ref, blocks_ref, start, size):
    width = weight_ref.shape[1] // (2 * NY)
    parts = [pl.ds(pl.multiple_of(blocks_ref[k] * width + start, 256), size) for k in range(NY)]
    return jnp.concatenate([weight_ref[:, p] for p in parts], axis=1)


def side_by_side(rows_ref, part):
    return jnp.concatenate([rows_ref[k, part, :] for k in range(rows_ref.shape[0])], axis=1)


def half_logits_kernel(block_ref, rows_ref, weight_ref, *refs, second, step):
    out_ref = refs[-1]
    half = rows_ref.shape[2]
    left = columns(weight_ref, block_ref, second * half, half)
    for i in range(0, out_ref.shape[1], step):
        part = dot(left, side_by_side(rows_ref, pl.ds(i, step)), 1, 1)
        out_ref[:, i : i + step] = part if len(refs) == 1 else refs[0][:, i : i + step] + part


def half_logits(blocks, second, rows, weight, *before):
    count, tokens, half = rows.shape
    width = weight.shape[0]
    body = functools.partial(half_logits_kernel, second=second, step=256)
    return call(
        body, "logits_half", array((width, tokens), f32), rows, weight, *before,
        prefetch=(blocks,), flops=2 * count * tokens * half * width, size=6 * 2**20,
    )


def logits_rest_kernel(block_ref, first_ref, second_ref, weight_ref, own_ref, dense_ref, out_ref, stats_ref, *, step):
    tokens, half = out_ref.shape[1], first_ref.shape[2]
    left = jnp.concatenate([columns(weight_ref, block_ref, h * half, half) for h in range(2)], axis=1)
    for i in range(0, tokens, step):
        here = pl.ds(i, step)
        right = jnp.concatenate([side_by_side(first_ref, here), side_by_side(second_ref, here)], axis=1)
        logits = own_ref[:, i : i + step] + dot(left, right, 1, 1)
        out_ref[:, i : i + step] = logits
        peak = jnp.max(logits, axis=0, keepdims=True)
        weights = jnp.exp(logits - peak)
        total = jnp.sum(weights, axis=0, keepdims=True)
        stats_ref[:, i : i + step] = peak + jnp.log(total)
        target = jnp.sum(logits * dense_ref[:, i : i + step], axis=0, keepdims=True)
        stats_ref[:, tokens + i : tokens + i + step] = target
        mean = jnp.sum(weights * logits, axis=0, keepdims=True) / total
        stats_ref[:, 2 * tokens + i : 2 * tokens + i + step] = mean


def logits_call(blocks, rows, weight, own, dense):
    count, tokens, half = rows[0].shape
    width = weight.shape[0]
    return call(
        functools.partial(logits_rest_kernel, step=256), "logits_rest",
        [array((width, tokens), f32), array((1, 3 * tokens), f32)], *rows, weight, own, dense,
        prefetch=(blocks,), flops=4 * count * tokens * half * width, size=8 * 2**20,
    )


def grad_kernel(
    block_ref, stats_ref, logits_ref, dense_ref, logprob_ref, weight_ref, grad_ref, turned_ref, out_ref, pad_ref
):
    width, tokens = logits_ref.shape
    step = pad_ref.shape[1]
    pad_ref[...] = jnp.zeros(pad_ref.shape, f32)
    for i in range(0, tokens, step):
        totals = stats_ref[:, i : i + step]
        peak = jnp.max(totals, axis=0, keepdims=True)
        total = peak + jnp.log(jnp.sum(jnp.exp(totals - peak), axis=0, keepdims=True))
        mass = jnp.sum(jnp.exp(logprob_ref[:, i : i + step]), axis=0, keepdims=True)
        student = mass * jnp.exp(logits_ref[:, i : i + step] - total)
        grad = loss_scale * (student - dense_ref[:, i : i + step])
        grad_ref[:, i : i + step] = grad.astype(bf16)
        pad_ref[:width, :] = grad
        turned_ref[i : i + step, :] = pad_ref[...].T[:, :width].astype(bf16)
    rest_kernel(block_ref, turned_ref, weight_ref, out_ref, second=0)


def feature_part(weight_ref, blocks_ref, k, second):
    half = weight_ref.shape[1] // (4 * NY)
    return weight_ref[:, pl.ds(pl.multiple_of(blocks_ref[k] * 2 * half + second * half, 256), half)]


def grad_call(blocks, stats, logits, dense, logprob, weight):
    width, tokens = logits.shape
    count = blocks.shape[0]
    half = weight.shape[1] // (4 * count)
    inside = pl.BlockSpec(memory_space=pltpu.VMEM)
    return call(
        grad_kernel, "grad_logits",
        [array((width, tokens), bf16), array((tokens, width), bf16), array((count, tokens, half), bf16)],
        stats, logits, dense, logprob, weight, prefetch=(blocks,), ins=[inside] * 5, outs=[inside] * 3,
        scratch=[pltpu.VMEM((-(-width // 128) * 128, 128), f32)],
        flops=2 * count * tokens * half * width, size=12 * 2**20,
    )


def rest_kernel(block_ref, turned_ref, weight_ref, out_ref, *, second):
    for k in range(out_ref.shape[0]):
        out_ref[k] = dot(turned_ref[...], feature_part(weight_ref, block_ref, k, second)).astype(bf16)


def add_kernel(block_ref, turned_ref, weight_ref, other_ref, out_ref, *, second):
    for k in range(out_ref.shape[0]):
        out = dot(turned_ref[...], feature_part(weight_ref, block_ref, k, second))
        out_ref[k] = (out + other_ref[k].astype(f32)).astype(bf16)


def split_kernel(block_ref, at_ref, turned_ref, weight_ref, other_ref, *refs, second):
    by_x, keep_ref = refs[:4], refs[4]
    rows = keep_ref.shape[2]
    for y in range(other_ref.shape[0]):
        out = dot(turned_ref[...], feature_part(weight_ref, block_ref, y, second))
        out = (out + other_ref[y].astype(f32)).astype(bf16)
        for k in range(4):
            keep_ref[k, y] = out[k * rows : (k + 1) * rows]
    for k in range(4):
        by_x[k][...] = keep_ref[(at_ref[0] + k) % 4]


def half_call(body, name, blocks, second, turned, weight, *other, at=None):
    tokens, width = turned.shape
    count = blocks.shape[0]
    half = weight.shape[1] // (4 * count)
    rows = tokens // NX
    inside = pl.BlockSpec(memory_space=pltpu.VMEM)
    if at is None:
        out, outs, scratch, prefetch = array((count, tokens, half), bf16), inside, (), (blocks,)
    else:
        out, outs = [array((count, rows, half), bf16)] * 4, [inside] * 4
        scratch, prefetch = [pltpu.VMEM((NX, count, rows, half), bf16)], (blocks, at)
    return call(
        functools.partial(body, second=second), name, out, turned, weight, *other, prefetch=prefetch, scratch=scratch,
        ins=[inside] * (2 + len(other)), outs=outs, flops=2 * count * tokens * half * width, size=6 * 2**20,
    )


def sum_kernel(at_ref, by_y_ref, *refs):
    by_x, to_x, to_y_ref, keep_ref = refs[:4], refs[4:8], refs[8], refs[9]
    count, rows = by_x[0].shape[:2]
    for i in range(count):
        part = pl.ds(i * rows, rows)
        keep_ref[i] = sum(by_y_ref[j, part, :].astype(f32) for j in range(count)).astype(bf16)
        to_y_ref[i] = sum(r[i].astype(f32) for r in by_x).astype(bf16)
    for k in range(4):
        to_x[k][...] = keep_ref[(at_ref[0] + k) % 4]


def tokens_kernel(stats_ref, logprob_ref, kl_ref, dots_ref):
    tokens = kl_ref.shape[1]
    logprob = logprob_ref[...]
    prob = jnp.exp(logprob)
    mass = jnp.sum(prob, axis=0, keepdims=True)
    totals = stats_ref[:, :tokens]
    peak = jnp.max(totals, axis=0, keepdims=True)
    weights = jnp.exp(totals - peak)
    total = jnp.sum(weights, axis=0, keepdims=True)
    target = jnp.sum(stats_ref[:, tokens : 2 * tokens], axis=0, keepdims=True)
    mean = jnp.sum(weights * stats_ref[:, 2 * tokens :], axis=0, keepdims=True) / total
    kl_ref[...] = jnp.sum(prob * logprob, axis=0, keepdims=True) - target + mass * (peak + jnp.log(total))
    dots_ref[...] = loss_scale * (mass * mean - target)


def spread_kernel(*refs):
    by_x, (by_y_ref, spread_ref, out_ref) = refs[:4], refs[4:]
    first = sum(r[...].astype(f32) for r in by_x)
    second = sum(by_y_ref[j].astype(f32) for j in range(by_y_ref.shape[0]))
    both = jnp.concatenate([first.astype(bf16), second.astype(bf16)], axis=1)
    slots, lanes = out_ref.shape[1:]
    turns = slots // NX
    for z in range(out_ref.shape[0] // NX):
        rows = dot(spread_ref[z * slots : (z + 1) * slots, :].astype(bf16), both).astype(bf16)
        for k in range(NX):
            for i in range(both.shape[1] // lanes):
                out_ref[z * NX + k, i * turns : (i + 1) * turns, :] = rows[
                    k * turns : (k + 1) * turns, i * lanes : (i + 1) * lanes
                ]


def finish_kernel(at_ref, got_ref, rows_ref, gain_ref, dots_ref, out_ref, sum_ref, grad_ref):
    offset, count = own_slots(at_ref)
    lanes, share = sum_ref.shape[2], grad_ref.shape[1]
    slots, features = rows_ref.shape
    turns = slots // NX
    tokens = dots_ref.shape[1]
    for k in range(NX):
        total = got_ref[k].astype(f32)
        for z in range(1, got_ref.shape[0] // NX):
            total += got_ref[z * NX + k].astype(f32)
        sum_ref[k] = total
    for i in range(NX):
        for m in range(turns):
            for j in range(share // lanes):
                row = j * turns + m
                grad_ref[NX * m + i : NX * m + i + 1, j * lanes : (j + 1) * lanes] = sum_ref[
                    (offset + i) & (NX - 1), row : row + 1, :
                ]
    rank = offset + lax.broadcasted_iota(jnp.int32, (slots, tokens), 0)
    row = (rank & (NX - 1)) * (tokens // NX) + ((rank & (GROUPS - 1)) >> 2) * (tokens // GROUPS) + (rank >> 5)
    here = row == lax.broadcasted_iota(jnp.int32, (slots, tokens), 1)
    dots = jnp.sum(jnp.where(here, dots_ref[...], 0.0), axis=1, keepdims=True)
    part = pl.ds(pl.multiple_of(at_ref[3] * share, share), share)
    inv_rms = inverse_rms(rows_ref, share)
    grad = (grad_ref[...] * gain_ref[:, part] - rows_ref[:, part].astype(f32) * (inv_rms * dots / features)) * inv_rms
    live = lax.broadcasted_iota(jnp.int32, grad.shape, 0) < count
    out_ref[...] = jnp.where(live, grad, 0.0).astype(bf16)


def weight_grad_kernel(block_ref, *refs):
    own, rest, grad_ref, out_ref = refs[:2], refs[2:4], refs[4], refs[5]

    def write(rows):
        half = rows[0].shape[2]
        for h in range(2):
            out_ref[:, h * half : (h + 1) * half] = dot(grad_ref[...], rows[h][0]).astype(bf16)

    count = pl.num_programs(0) // 2

    @pl.when(pl.program_id(0) < count)
    def _():
        write(own)

    @pl.when(pl.program_id(0) >= count)
    def _():
        write(rest)


def weight_grad(blocks, own, rest, grad):
    count, tokens, half = own[0].shape
    width = grad.shape[0]
    return call(
        weight_grad_kernel, "weight_grad", array((width, 4 * count * half), bf16), *own, *rest, grad,
        grid=(2 * count,), prefetch=(blocks,),
        ins=[
            *[pl.BlockSpec((1, tokens, half), lambda k, b: (jnp.minimum(k, count - 1), 0, 0))] * 2,
            *[pl.BlockSpec((1, tokens, half), lambda k, b: (jnp.maximum(k - count, 0), 0, 0))] * 2,
            pl.BlockSpec((width, tokens), lambda k, b: (0, 0)),
        ],
        outs=pl.BlockSpec((width, 2 * half), lambda k, b: (0, b[k])),
        flops=8 * count * tokens * half * width, size=16 * 2**20,
    )


def after(small, *others):
    return lax.optimization_barrier((small, others))[0]


def exchange(x, axis, lines=None):
    return lax.all_to_all(x, axis, 0, 0, tiled=True, axis_index_groups=lines)


def along_x(x, k):
    return lax.ppermute(x, "seq", [(i, i // NX * NX + (i + k) % NX) for i in range(GROUPS)])


def along_y(x, k):
    return lax.ppermute(x, "vocab", [(i, (i + 2 * k) % (2 * NY)) for i in range(2 * NY)])


def from_ahead(x, move):
    got = {k: move(x, -k) for k in STEPS}
    return [x, got[1], got[2], got[3]]


def to_ahead(pieces, move):
    return [pieces[0], *(move(pieces[k], k) for k in STEPS)]


def merge(stats):
    tokens = stats[0].shape[1] // 3
    totals = [s[:, :tokens] for s in stats]
    peak = totals[0]
    for t in totals[1:]:
        peak = jnp.maximum(peak, t)
    weights = [jnp.exp(t - peak) for t in totals]
    total = sum(weights)
    target = sum(s[:, tokens : 2 * tokens] for s in stats)
    mean = sum(w * s[:, 2 * tokens :] for w, s in zip(weights, stats)) / total
    return jnp.concatenate([peak + jnp.log(total), target, mean], axis=1)


def per_device(rollout, group_count, final_gain, head_weight, teacher_index, teacher_logprob):
    slots, features = rollout.shape
    tokens, entries = teacher_index.shape
    width = head_weight.shape[1]
    weight = head_weight.T
    parts = 2 * NY
    share = features // parts
    half = share // 2
    class_rows = tokens // NX
    turns = slots // NX
    pack_rows = tokens // GROUPS
    seq = lax.axis_index("seq")
    own_z, own_x = seq // NX, seq % NX
    vocab = lax.axis_index("vocab")
    own_y, core = vocab // 2, vocab % 2
    at = jnp.concatenate([jnp.stack([own_x, own_y, seq, vocab]).astype(jnp.int32), group_count])

    of_class = call(
        sort_kernel, "sort_rows", array((GROUPS, slots, share // NX), bf16), rollout, final_gain[None, :], prefetch=(at,), size=2**19
    )
    of_class = exchange(of_class, "seq")

    def class_order(a):
        return a.reshape(NZ, NX, pack_rows, entries).transpose(1, 0, 2, 3).reshape(tokens, entries).T

    index = class_order(teacher_index)
    logprob = class_order(teacher_logprob)
    first_column = (seq * parts + vocab) * width
    dense = teacher_columns(first_column, index, logprob, width)

    group_ids = jnp.arange(GROUPS, dtype=jnp.int32)
    before = group_ids[None, :] < group_ids[:, None]
    offsets = jnp.sum(jnp.where(before, group_count[None, :], 0), axis=1)
    turn_ids = jnp.arange(turns, dtype=jnp.int32)
    row_in_group = (own_x - offsets[:, None]) % NX + NX * turn_ids[None, :]
    rank = offsets[:, None] + row_in_group
    place = jnp.where(row_in_group < group_count[:, None], rank % GROUPS // NX * pack_rows + rank // GROUPS, class_rows)
    place_ids = jnp.arange(class_rows, dtype=jnp.int32)
    place = after(place, dense)
    spread = lax.optimization_barrier((place.reshape(-1, 1) == place_ids[None, :]).astype(f32))
    inside = pl.BlockSpec(memory_space=pltpu.VMEM)
    own_first, own_second = call(
        compact_kernel, "compact", [array((class_rows, half), bf16), array((NY, class_rows, half), bf16)],
        of_class, spread, ins=[inside] * 2, outs=[inside] * 2,
        scratch=[pltpu.VMEM((GROUPS * turns, share), f32)], size=2**20,
    )

    by_x = from_ahead(own_first, along_x)
    all_y = exchange(own_second, "vocab", Y_LINES)
    all_x = call(place_kernel, "place", array((NY, NX, class_rows, half), bf16), *by_x, prefetch=(at,), size=2**21)
    by_x = from_ahead(all_y, along_x)
    own_first = exchange(all_x.reshape(NY, tokens, half), "vocab", Y_LINES)

    y_ids = jnp.arange(NY, dtype=jnp.int32)
    own_blocks = 2 * y_ids + core
    rest_blocks = 2 * y_ids + 1 - core
    own_second = call(
        gather_kernel, "gather_rows", array((NY, NX, class_rows, half), bf16), *by_x, prefetch=(at,), size=2**22
    ).reshape(NY, tokens, half)
    rest_second = lax.ppermute(own_second, "vocab", OTHER_CORE)
    logits_own = half_logits(own_blocks, 1, own_second, weight)
    rest_first = lax.ppermute(own_first, "vocab", OTHER_CORE)
    logits_own = half_logits(after(own_blocks, logits_own), 0, own_first, weight, logits_own)
    own_rows, rest_rows = [own_first, own_second], [rest_first, rest_second]
    logits, stats = logits_call(rest_blocks, rest_rows, weight, logits_own, dense)
    stats = merge([stats, lax.ppermute(stats, "vocab", OTHER_CORE)])
    stats = merge(from_ahead(stats, along_y))
    stats = exchange(jnp.broadcast_to(stats, (GROUPS, 3 * tokens)), "seq")

    grad, turned, rest_first = grad_call(rest_blocks, stats, logits, dense, logprob, weight)
    other_first = lax.ppermute(rest_first, "vocab", OTHER_CORE)
    other_second = lax.ppermute(half_call(rest_kernel, "grad_rest", rest_blocks, 1, turned, weight), "vocab", OTHER_CORE)
    first = half_call(add_kernel, "grad_first", own_blocks, 0, turned, weight, other_first)
    by_y = exchange(first, "vocab", Y_LINES)
    pieces = half_call(split_kernel, "grad_second", after(own_blocks, first), 1, turned, weight, other_second, at=at)
    by_x = to_ahead(pieces, along_x)
    weight_t = weight_grad(after(jnp.concatenate([own_blocks, rest_blocks]), pieces), own_rows, rest_rows, grad)
    kl, dots = call(tokens_kernel, "tokens", [array((1, tokens), f32)] * 2, stats, logprob, size=2**19)
    kl = lax.dynamic_slice_in_dim(kl[0], own_x * class_rows + own_z * pack_rows, pack_rows)
    at = after(at, weight_t, kl, dots)

    small = array((class_rows, half), bf16)
    inside = pl.BlockSpec(memory_space=pltpu.VMEM)
    *pieces, to_y = call(
        sum_kernel, "add_pieces", [small] * 4 + [array((NY, class_rows, half), bf16)], by_y, *by_x, prefetch=(at,),
        ins=[inside] * 5, outs=[inside] * 5, scratch=[pltpu.VMEM((NX, class_rows, half), bf16)], size=2**22,
    )
    by_x = to_ahead(pieces, along_x)
    by_y = exchange(to_y, "vocab", Y_LINES)
    spread_grad = call(
        spread_kernel, "spread_rows", array((GROUPS, slots, share // NX), bf16), *by_x, by_y, spread, size=2**20
    )
    grad_rollout = call(
        finish_kernel, "finish", array((slots, share), bf16), exchange(spread_grad, "seq"), rollout, final_gain[None, :],
        dots, prefetch=(at,), ins=[inside] * 4, outs=inside,
        scratch=[pltpu.VMEM((NX, slots, share // NX), f32), pltpu.VMEM((slots, share), f32)], size=2**19,
    )
    return (kl, weight_t.T, grad_rollout)


def solution(mesh):
    placed = (P("seq", None), P(), P(), P(None, ("seq", "vocab")), P(), P())
    return jax.shard_map(
        per_device,
        mesh=mesh,
        in_specs=placed,
        out_specs=(P("seq"), P(None, ("seq", "vocab")), P("seq", "vocab")),
        check_vma=False,
    )
```
